512 devices in a mesh: patch: 128 (over y, x, z_lo), head: 4 (over z_hi, core).
Axes of the slice: x: 4, y: 4, z: 16 (z_hi: 2, z_lo: 8; z = z_hi * 8 + z_lo), core: 2. Of those that a mesh axis runs over, the one named last changes fastest.
Arguments:
- q_fresh: bfloat16 [65536, 1536], P(('patch', 'head')), may hold values from -8 to 8
- k_fresh: bfloat16 [65536, 1536], P(('patch', 'head')), may hold values from -8 to 8
- v_fresh: bfloat16 [65536, 1536], P(('patch', 'head')), may hold values from -6 to 6
- k_stale: bfloat16 [2048, 1536], P('patch', 'head'), may hold values from -8 to 8
- v_stale: bfloat16 [2048, 1536], P('patch', 'head'), may hold values from -6 to 6
Outputs:
- attended: bfloat16 [65536, 1536], P(('patch', 'head'))
The draws below stay inside these ranges and needn't reach their ends.
All inputs are finite; a program needn't handle non-finite values.
Results may differ from the reference program's by a relative error of at most 0.0045.
Values may be sent and summed in bfloat16 or wider, within the bound.
No kernel may reach another device: no remote copies, remote signals or barrier semaphores. Data moves between devices by JAX's collectives and lax.ppermute only.
A program may use at most 64 MiB of HBM per device.

```python
import jax
import jax.numpy as jnp
from jax import lax

HEADS = 12
HD = 128
POOLED = 16
WH = 1536
TOK_PATCH = 512
TOKENS = 65536
STALE = 2048
N_PATCH = 128


def draw_q_fresh(key, part):
    key = jax.random.fold_in(key, 11)
    values = jnp.clip(1.7 * jax.random.normal(key, (TOKENS, WH), jnp.float32), -8.0, 8.0)
    return values.astype(jnp.bfloat16)


def draw_k_stale(key, part):
    key = jax.random.fold_in(key, 23)
    values = jnp.clip(1.7 * jax.random.normal(key, (STALE, WH), jnp.float32), -8.0, 8.0)
    return values.astype(jnp.bfloat16)


def shard_levels(key, shape, cuts, smallest, largest):
    loudness = 1.0
    for axis_at, blocks in cuts:
        draws = jax.random.uniform(jax.random.fold_in(jax.random.fold_in(key, 6), axis_at), (blocks,), jnp.float32, smallest / len(cuts), largest / len(cuts))
        loudness = loudness * jnp.repeat(jnp.exp(draws), shape[axis_at] // blocks).reshape((-1,) + (1,) * (len(shape) - 1 - axis_at))
    return loudness


def bell_draw(rng, dims, spread, reach, shards=(), kind=jnp.bfloat16):
    level = shard_levels(rng, dims, shards, -0.22, 0.18) if shards else 1.0
    values = jax.random.normal(rng, dims, jnp.float32) * spread * level
    return jnp.minimum(jnp.maximum(values, -reach), reach).astype(kind)


def setup_inputs(seed: int = 0) -> dict:
    key_list = jax.random.split(jax.random.key(seed), 6)
    q_fresh = draw_q_fresh(jax.random.fold_in(key_list[5], 71), 0)
    k_fresh = bell_draw(key_list[1], (TOKENS, WH), 1.7, 8.0, ((0, 512),))
    v_fresh = bell_draw(key_list[2], (TOKENS, WH), 1.0, 6.0, ((0, 512),))
    k_stale = draw_k_stale(jax.random.fold_in(key_list[5], 71), 0)
    v_stale = bell_draw(key_list[4], (STALE, WH), 1.0, 6.0, ((0, 128), (1, 4)))
    return dict(q_fresh=q_fresh, k_fresh=k_fresh, v_fresh=v_fresh, k_stale=k_stale, v_stale=v_stale)


def reference(q_fresh, k_fresh, v_fresh, k_stale, v_stale):
    scaling = HD ** -0.5
    stale_group = jnp.arange(STALE, dtype=jnp.int32) // POOLED

    def one_patch(patch_index):
        first_row = (patch_index * TOK_PATCH).astype(jnp.int32)
        fresh_keys = lax.dynamic_slice_in_dim(k_fresh, first_row, TOK_PATCH, 0)
        fresh_values = lax.dynamic_slice_in_dim(v_fresh, first_row, TOK_PATCH, 0)
        all_keys = jnp.concatenate([fresh_keys, k_stale], axis=0)
        all_values = jnp.concatenate([fresh_values, v_stale], axis=0)
        kept = jnp.concatenate([jnp.ones((TOK_PATCH,), jnp.bool_), stale_group != patch_index.astype(jnp.int32)])
        queries = lax.dynamic_slice_in_dim(q_fresh, first_row, TOK_PATCH, 0)
        queries = queries.reshape(TOK_PATCH, HEADS, HD).astype(jnp.float32)
        key_heads = all_keys.reshape(TOK_PATCH + STALE, HEADS, HD).astype(jnp.float32)
        value_heads = all_values.reshape(TOK_PATCH + STALE, HEADS, HD).astype(jnp.float32)
        scores = jnp.einsum("qhd,khd->hqk", queries, key_heads) * scaling
        scores = jnp.where(kept[None, None, :], scores, -jnp.inf)
        top_score = jnp.max(scores, axis=2, keepdims=True)
        weights = jnp.exp(scores - top_score)
        totals = jnp.sum(weights, axis=2)
        rounded = lax.optimization_barrier(weights.astype(jnp.bfloat16)).astype(jnp.float32)
        mixed = jnp.einsum("hqk,khd->qhd", rounded, value_heads)
        attended = mixed / jnp.transpose(totals)[:, :, None]
        return attended.reshape(TOK_PATCH, WH).astype(jnp.bfloat16)

    return lax.map(one_patch, jnp.arange(N_PATCH, dtype=jnp.int32)).reshape(TOKENS, WH)
```

```python
import functools
import math

import jax
import jax.numpy as jnp
import numpy as np
from jax import lax
from jax.experimental import pallas as pl
from jax.experimental.pallas import tpu as pltpu
from jax.sharding import Mesh
from jax.sharding import PartitionSpec as P

HD = 128
EVERY = ("y", "x", "zl", "zh", "core")
SIZES = (4, 4, 8, 2, 2)
ROWS = 128
SCALE = HD**-0.5 * math.log2(math.e)
NT = (((1,), (1,)), ((), ()))
F32 = jnp.float32


def weigh(own_ref, q_ref, k_ref, *refs):
    keys, values = refs[0:4], refs[4:8]
    acc_ref, fresh_ref, total_ref, s_ref = refs[8:12]
    heads = q_ref.shape[1] // HD
    fresh = k_ref.shape[0]
    block = keys[0].shape[0] // 4
    first = own_ref[0]
    cols = lax.broadcasted_iota(jnp.int32, (ROWS, block), 1)
    own = (cols >= first) & (cols < first + 16)
    lane = lax.broadcasted_iota(jnp.int32, (ROWS, HD), 1)

    def rows_step(i, carry):
        rows = pl.ds(pl.multiple_of(i * ROWS, ROWS), ROWS)
        totals = jnp.zeros((ROWS, HD), F32)
        for h in range(heads):
            cs = slice(h * HD, (h + 1) * HD)
            q = q_ref[rows, cs]
            top = jnp.full((ROWS, HD), -jnp.inf, F32)
            for dy in range(4):
                s = lax.dot_general(q, keys[dy][:, cs], NT, preferred_element_type=F32)
                for dx in range(4):
                    part = s[:, dx * block : (dx + 1) * block]
                    if dy == 0 and dx == 0:
                        part = jnp.where(own, -jnp.inf, part)
                    at = (dx * 4 + dy) * block
                    s_ref[h, :, at : at + block] = part
                    top = jnp.maximum(top, part)
            s = lax.dot_general(q, k_ref[:, cs], NT, preferred_element_type=F32)
            s_ref[h, :, 16 * block :] = s
            for c in range(0, fresh, HD):
                top = jnp.maximum(top, s[:, c : c + HD])
            top = jnp.max(top, axis=1, keepdims=True) * SCALE
            sums = jnp.zeros((ROWS, HD), F32)
            acc = jnp.zeros((ROWS, HD), F32)
            for dx in range(5):
                width = 4 * block if dx < 4 else fresh
                w = jnp.exp2(s_ref[h, :, dx * 4 * block : dx * 4 * block + width] * SCALE - top)
                for c in range(0, width, HD):
                    sums = sums + w[:, c : c + HD]
                rounded = w.astype(jnp.bfloat16)
                if dx < 4:
                    acc = acc + jnp.dot(rounded, values[dx][:, cs], preferred_element_type=F32)
                else:
                    fresh_ref[h, rows, :] = rounded
            acc_ref[rows, cs] = acc
            total = jnp.sum(sums, axis=1, keepdims=True)
            totals = jnp.where(lane == h, total, totals)
        total_ref[rows, :] = totals
        return carry

    lax.fori_loop(0, q_ref.shape[0] // ROWS, rows_step, 0)


def finish(v_ref, acc_ref, fresh_ref, total_ref, out_ref):
    for h in range(acc_ref.shape[1] // HD):
        cs = slice(h * HD, (h + 1) * HD)
        acc = acc_ref[:, cs] + jnp.dot(fresh_ref[h], v_ref[:, cs], preferred_element_type=F32)
        out_ref[:, cs] = (acc / total_ref[:, h : h + 1]).astype(out_ref.dtype)


def moves(axis, step):
    pairs = []
    at = EVERY.index(axis)
    for i in range(math.prod(SIZES)):
        place = list(np.unravel_index(i, SIZES))
        place[at] = (place[at] - step) % SIZES[at]
        pairs.append((i, int(np.ravel_multi_index(place, SIZES))))
    return pairs


def ring(block, axis):
    return [block] + [lax.ppermute(block, EVERY, moves(axis, d)) for d in (1, 2, 3)]


def swap(rows_of):
    return lax.all_to_all(rows_of, ("zh", "core"), split_axis=0, concat_axis=0, tiled=False)


def local(q_fresh, k_fresh, v_fresh, k_stale, v_stale):
    tokens, width = q_fresh.shape
    mine = k_stale.shape[1]
    pooled = k_stale.shape[0]
    heads = mine // HD
    both = jnp.concatenate([k_stale, v_stale], axis=1)
    line = lax.all_to_all(
        jnp.broadcast_to(both[None], (8, pooled, 2 * mine)), "zl", split_axis=0, concat_axis=0
    ).reshape(8 * pooled, 2 * mine)

    def to_heads(a):
        return swap(a.reshape(tokens, 4, mine).transpose(1, 0, 2)).reshape(4 * tokens, mine)

    q, k, v = to_heads(q_fresh), to_heads(k_fresh), to_heads(v_fresh)
    keys = ring(jnp.concatenate(ring(line[:, :mine], "x"), axis=0), "y")
    values = ring(jnp.concatenate(ring(line[:, mine:], "y"), axis=0), "x")
    own = (lax.axis_index("zl") * pooled).astype(jnp.int32).reshape(1)

    n, f = 4 * tokens, k.shape[0]
    vm = pl.BlockSpec(memory_space=pltpu.VMEM)
    total_keys = 16 * 8 * pooled + f
    acc, fresh, totals = pl.pallas_call(
        weigh,
        out_shape=(
            jax.ShapeDtypeStruct((n, mine), F32),
            jax.ShapeDtypeStruct((heads, n, f), jnp.bfloat16),
            jax.ShapeDtypeStruct((n, HD), F32),
        ),
        in_specs=[pl.BlockSpec(memory_space=pltpu.SMEM)] + [vm] * 10,
        out_specs=(vm, vm, vm),
        scratch_shapes=[pltpu.VMEM((heads, ROWS, total_keys), F32)],
        compiler_params=pltpu.CompilerParams(vmem_limit_bytes=40 << 20),
        cost_estimate=pl.CostEstimate(
            flops=4 * n * heads * total_keys * HD, bytes_accessed=10 << 20, transcendentals=n * heads * total_keys
        ),
        name="weigh",
    )(own, q, k, *keys, *values)
    out = pl.pallas_call(
        finish,
        out_shape=jax.ShapeDtypeStruct((n, mine), jnp.bfloat16),
        in_specs=[vm] * 4,
        out_specs=vm,
        compiler_params=pltpu.CompilerParams(vmem_limit_bytes=40 << 20),
        cost_estimate=pl.CostEstimate(flops=2 * n * heads * f * HD, bytes_accessed=4 << 20, transcendentals=0),
        name="finish",
    )(v, acc, fresh, totals)
    return swap(out.reshape(4, tokens, mine)).transpose(1, 0, 2).reshape(tokens, width)


def solution(mesh):
    fine = Mesh(mesh.devices.reshape(SIZES), EVERY)
    whole = P(EVERY, None)
    part = P(("y", "x", "zl"), ("zh", "core"))
    return jax.shard_map(
        local,
        mesh=fine,
        in_specs=(whole, whole, whole, part, part),
        out_specs=whole,
        check_vma=False,
    )
```

```python
import math

import jax
import jax.numpy as jnp
import numpy as np
from jax import lax
from jax.experimental import pallas as pl
from jax.experimental.pallas import tpu as pltpu
from jax.sharding import Mesh
from jax.sharding import PartitionSpec as P

HD = 128
EVERY = ("y", "x", "zl", "zh", "core")
SIZES = (4, 4, 8, 2, 2)
ROWS = 128
SCALE = HD**-0.5 * math.log2(math.e)
NT = (((1,), (1,)), ((), ()))
F32 = jnp.float32
BF16 = jnp.bfloat16
ANY = pl.BlockSpec(memory_space=pl.ANY)
SMEM = pl.BlockSpec(memory_space=pltpu.SMEM)


def pack(at_ref, q_ref, k_ref, v_ref, ks_ref, vs_ref, *refs):
    parts, pooled_ref, sem = refs[0:4], refs[4], refs[5]
    mine = ks_ref.shape[1]
    copies = []
    for j in range(pooled_ref.shape[0]):
        copies.append((ks_ref, pooled_ref.at[j, :, 0:mine]))
        copies.append((vs_ref, pooled_ref.at[j, :, mine : 2 * mine]))
    for p, part in enumerate(parts):
        cols = pl.ds(pl.multiple_of(at_ref[p] * mine, HD), mine)
        for t, ref in enumerate((q_ref, k_ref, v_ref)):
            copies.append((ref.at[:, cols], part.at[:, t * mine : (t + 1) * mine]))
    copies = [pltpu.make_async_copy(a, b, sem.at[i]) for i, (a, b) in enumerate(copies)]
    for c in copies:
        c.start()
    for c in copies:
        c.wait()


def attend(at_ref, p0, p1, p2, p3, pool_ref, out_ref, part_ref, keys_ref, s_ref, res_ref, sem_p, sem_k, sem_o):
    tokens = p0.shape[0]
    mine = p0.shape[1] // 3
    heads = mine // HD
    blocks, block = pool_ref.shape[0], pool_ref.shape[1]
    here = at_ref[5]
    loads = [pltpu.make_async_copy(r, part_ref.at[i], sem_p.at[i]) for i, r in enumerate((p0, p1, p2, p3))]
    for c in loads:
        c.start()
    for j in range(blocks):
        pltpu.make_async_copy(
            pool_ref.at[lax.rem(here + j, blocks)], keys_ref.at[pl.ds(j * block, block)], sem_k.at[j]
        ).start()
    for c in loads:
        c.wait()
    for j in range(blocks):
        pltpu.make_async_copy(pool_ref.at[0], keys_ref.at[pl.ds(j * block, block)], sem_k.at[j]).wait()
    first = at_ref[4]
    cols = lax.broadcasted_iota(jnp.int32, (ROWS, block), 1)
    own = (cols >= first) & (cols < first + 16)
    chunk = 512
    stale = blocks * block

    def rows_step(i, carry):
        for h in range(heads):
            cs = slice(h * HD, (h + 1) * HD)
            ks = slice(mine + h * HD, mine + (h + 1) * HD)
            vs = slice(2 * mine + h * HD, 2 * mine + (h + 1) * HD)
            vcs = slice(mine + h * HD, mine + (h + 1) * HD)
            q = part_ref[i, :, cs]
            top = jnp.full((ROWS, HD), -jnp.inf, F32)
            for c in range(0, stale, chunk):
                s = lax.dot_general(q, keys_ref[c : c + chunk, cs], NT, preferred_element_type=F32)
                for d in range(0, chunk, HD):
                    piece = s[:, d : d + HD]
                    if c + d == 0:
                        piece = jnp.where(own, -jnp.inf, piece)
                    s_ref[h, :, c + d : c + d + HD] = piece
                    top = jnp.maximum(top, piece)
            for p in range(4):
                s = lax.dot_general(q, part_ref[p, :, ks], NT, preferred_element_type=F32)
                s_ref[h, :, stale + p * tokens : stale + (p + 1) * tokens] = s
                top = jnp.maximum(top, s)
            top = jnp.max(top, axis=1, keepdims=True) * SCALE
            sums = jnp.zeros((ROWS, HD), F32)
            acc = jnp.zeros((ROWS, HD), F32)
            for c in range(0, stale + 4 * tokens, chunk):
                w = jnp.exp2(s_ref[h, :, c : c + chunk] * SCALE - top)
                for d in range(0, chunk, HD):
                    sums = sums + w[:, d : d + HD]
                rounded = w.astype(BF16)
                if c < stale:
                    values = keys_ref[c : c + chunk, vcs]
                else:
                    values = jnp.concatenate([part_ref[p, :, vs] for p in range(4)], axis=0)
                acc = acc + jnp.dot(rounded, values, preferred_element_type=F32)
            total = jnp.sum(sums, axis=1, keepdims=True)
            res_ref[i, :, cs] = (acc / total).astype(BF16)
        pltpu.make_async_copy(res_ref.at[i], out_ref.at[at_ref[i]], sem_o.at[i]).start()
        return carry

    lax.fori_loop(0, 4, rows_step, 0)
    for i in range(4):
        pltpu.make_async_copy(res_ref.at[i], out_ref.at[0], sem_o.at[i]).wait()


def flips(zh, core):
    pairs = []
    for i in range(math.prod(SIZES)):
        place = list(np.unravel_index(i, SIZES))
        place[3] ^= zh
        place[4] ^= core
        pairs.append((i, int(np.ravel_multi_index(place, SIZES))))
    return pairs


def local(q_fresh, k_fresh, v_fresh, k_stale, v_stale):
    tokens, width = q_fresh.shape
    pooled, mine = k_stale.shape
    heads = mine // HD
    zh, core = lax.axis_index("zh"), lax.axis_index("core")
    zl, here = lax.axis_index("zl"), lax.axis_index("y") * 4 + lax.axis_index("x")
    places = [zh * 2 + core, zh * 2 + 1 - core, (1 - zh) * 2 + core, (1 - zh) * 2 + 1 - core, zl * pooled, here]
    at = jnp.stack(places).astype(jnp.int32)

    part = jax.ShapeDtypeStruct((tokens, 3 * mine), BF16)
    *parts, copies = pl.pallas_call(
        pack,
        out_shape=(part, part, part, part, jax.ShapeDtypeStruct((8, pooled, 2 * mine), BF16)),
        in_specs=[SMEM] + [ANY] * 5,
        out_specs=(ANY,) * 5,
        scratch_shapes=[pltpu.SemaphoreType.DMA((28,))],
        cost_estimate=pl.CostEstimate(flops=0, bytes_accessed=3 << 20, transcendentals=0),
        name="pack",
    )(at, q_fresh, k_fresh, v_fresh, k_stale, v_stale)
    line = lax.all_to_all(copies, "zl", split_axis=0, concat_axis=0).reshape(8 * pooled, 2 * mine)
    arrived = [
        parts[0],
        lax.ppermute(parts[1], EVERY, flips(0, 1)),
        lax.ppermute(parts[2], EVERY, flips(1, 0)),
        lax.ppermute(parts[3], EVERY, flips(1, 1)),
    ]
    pool = lax.all_to_all(
        jnp.broadcast_to(line[None], (16, 8 * pooled, 2 * mine)), ("y", "x"), split_axis=0, concat_axis=0
    )
    total_keys = 16 * 8 * pooled + 4 * tokens
    out = pl.pallas_call(
        attend,
        out_shape=jax.ShapeDtypeStruct((4, tokens, mine), BF16),
        in_specs=[SMEM] + [ANY] * 5,
        out_specs=ANY,
        scratch_shapes=[
            pltpu.VMEM((4, tokens, 3 * mine), BF16),
            pltpu.VMEM((16 * 8 * pooled, 2 * mine), BF16),
            pltpu.VMEM((heads, ROWS, total_keys), F32),
            pltpu.VMEM((4, tokens, mine), BF16),
            pltpu.SemaphoreType.DMA((4,)),
            pltpu.SemaphoreType.DMA((16,)),
            pltpu.SemaphoreType.DMA((4,)),
        ],
        compiler_params=pltpu.CompilerParams(vmem_limit_bytes=40 << 20),
        cost_estimate=pl.CostEstimate(
            flops=4 * 4 * tokens * heads * total_keys * HD,
            bytes_accessed=6 << 20,
            transcendentals=4 * tokens * heads * total_keys,
        ),
        name="attend",
    )(at, *arrived, pool)
    back = lax.all_to_all(out, ("zh", "core"), split_axis=0, concat_axis=0)
    return back.transpose(1, 0, 2).reshape(tokens, width)


def solution(mesh):
    fine = Mesh(mesh.devices.reshape(SIZES), EVERY)
    whole = P(EVERY, None)
    part = P(("y", "x", "zl"), ("zh", "core"))
    return jax.shard_map(
        local,
        mesh=fine,
        in_specs=(whole, whole, whole, part, part),
        out_specs=whole,
        check_vma=False,
    )
```

```python
import math

import jax
import jax.numpy as jnp
import numpy as np
from jax import lax
from jax.experimental import pallas as pl
from jax.experimental.pallas import tpu as pltpu
from jax.sharding import Mesh
from jax.sharding import PartitionSpec as P

HD = 128
EVERY = ("y", "x", "zl", "zh", "core")
SIZES = (4, 4, 8, 2, 2)
ROWS = 128
SCALE = HD**-0.5 * math.log2(math.e)
NT = (((1,), (1,)), ((), ()))
F32 = jnp.float32
BF16 = jnp.bfloat16
ANY = pl.BlockSpec(memory_space=pl.ANY)
SMEM = pl.BlockSpec(memory_space=pltpu.SMEM)


def pack(at_ref, qa, ka, va, ksa, vsa, own_ref, near_ref, qz_ref, kvz_ref, pooled_ref, *scratch):
    q_ref, k_ref, v_ref, ks_ref, vs_ref, sem = scratch
    loads = zip((qa, ka, va, ksa, vsa), scratch[:5])
    loads = [pltpu.make_async_copy(a, b, sem.at[i]) for i, (a, b) in enumerate(loads)]
    for c in loads:
        c.start()
    for c in loads:
        c.wait()
    mine = ks_ref.shape[1]

    def cols(p):
        return pl.ds(pl.multiple_of(at_ref[p] * mine, HD), mine)

    for t, ref in enumerate((q_ref, k_ref, v_ref)):
        own_ref[:, t * mine : (t + 1) * mine] = ref[:, cols(0)]
        near_ref[:, t * mine : (t + 1) * mine] = ref[:, cols(1)]
    for r in range(2):
        qz_ref[r] = q_ref[:, cols(2 + r)]
        kvz_ref[r, :, 0:mine] = k_ref[:, cols(2 + r)]
        kvz_ref[r, :, mine : 2 * mine] = v_ref[:, cols(2 + r)]
    for j in range(pooled_ref.shape[0]):
        pooled_ref[j, :, 0:mine] = ks_ref[...]
        pooled_ref[j, :, mine : 2 * mine] = vs_ref[...]


def spread(line_ref, near_ref, qz_ref, out_ref):
    out_ref[0] = line_ref[...]


def attend(at_ref, own_ref, near_ref, qz_ref, kvz_ref, qc_ref, kvc_ref, pool_ref, out_ref, *scratch):
    q_ref, keys_ref, values_ref, s_ref, res_ref, sem_f, sem_k, sem_o = scratch
    tokens, mine = res_ref.shape[1:]
    heads = mine // HD
    blocks, block = pool_ref.shape[0], pool_ref.shape[1]
    stale = blocks * block
    here = at_ref[5]
    fresh = []
    for i, ref in enumerate((own_ref, near_ref)):
        fresh += [(i, t, ref.at[:, t * mine : (t + 1) * mine]) for t in range(3)]
    fresh += [(2, 0, qz_ref.at[0]), (2, 1, kvz_ref.at[0, :, 0:mine]), (2, 2, kvz_ref.at[0, :, mine : 2 * mine])]
    fresh += [(3, 0, qc_ref.at[1]), (3, 1, kvc_ref.at[1, :, 0:mine]), (3, 2, kvc_ref.at[1, :, mine : 2 * mine])]
    loads = []
    for n, (i, t, ref) in enumerate(fresh):
        rows = pl.ds(stale + i * tokens, tokens)
        to = (q_ref.at[i], keys_ref.at[rows], values_ref.at[rows])[t]
        loads.append(pltpu.make_async_copy(ref, to, sem_f.at[n]))
    for j in range(blocks):
        src = pool_ref.at[lax.rem(here + j, blocks)]
        rows = pl.ds(j * block, block)
        loads.append(pltpu.make_async_copy(src.at[:, 0:mine], keys_ref.at[rows], sem_k.at[j]))
        loads.append(pltpu.make_async_copy(src.at[:, mine : 2 * mine], values_ref.at[rows], sem_k.at[blocks + j]))
    for c in loads:
        c.start()
    for c in loads:
        c.wait()
    first = at_ref[4]
    cols = lax.broadcasted_iota(jnp.int32, (ROWS, block), 1)
    own = (cols >= first) & (cols < first + 16)
    chunk = 512
    total_keys = keys_ref.shape[0]

    def rows_step(i, carry):
        for h in range(heads):
            cs = slice(h * HD, (h + 1) * HD)
            q = q_ref[i, :, cs]
            top = jnp.full((ROWS, HD), -jnp.inf, F32)
            for c in range(0, total_keys, chunk):
                s = lax.dot_general(q, keys_ref[c : c + chunk, cs], NT, preferred_element_type=F32)
                for d in range(0, chunk, HD):
                    piece = s[:, d : d + HD]
                    if c + d == 0:
                        piece = jnp.where(own, -jnp.inf, piece)
                    s_ref[h, :, c + d : c + d + HD] = piece
                    top = jnp.maximum(top, piece)
            top = jnp.max(top, axis=1, keepdims=True) * SCALE
            sums = jnp.zeros((ROWS, HD), F32)
            acc = jnp.zeros((ROWS, HD), F32)
            for c in range(0, total_keys, chunk):
                w = jnp.exp2(s_ref[h, :, c : c + chunk] * SCALE - top)
                for d in range(0, chunk, HD):
                    sums = sums + w[:, d : d + HD]
                acc = acc + jnp.dot(w.astype(BF16), values_ref[c : c + chunk, cs], preferred_element_type=F32)
            total = jnp.sum(sums, axis=1, keepdims=True)
            res_ref[i, :, cs] = (acc / total).astype(BF16)
        pltpu.make_async_copy(res_ref.at[i], out_ref.at[at_ref[i]], sem_o.at[i]).start()
        return carry

    lax.fori_loop(0, 4, rows_step, 0)
    for i in range(4):
        pltpu.make_async_copy(res_ref.at[i], out_ref.at[0], sem_o.at[i]).wait()


def flips(zh, core):
    pairs = []
    for i in range(math.prod(SIZES)):
        place = list(np.unravel_index(i, SIZES))
        place[3] ^= zh
        place[4] ^= core
        pairs.append((i, int(np.ravel_multi_index(place, SIZES))))
    return pairs


def local(q_fresh, k_fresh, v_fresh, k_stale, v_stale):
    tokens, width = q_fresh.shape
    pooled, mine = k_stale.shape
    heads = mine // HD
    zh, core = lax.axis_index("zh"), lax.axis_index("core")
    zl, here = lax.axis_index("zl"), lax.axis_index("y") * 4 + lax.axis_index("x")
    places = [zh * 2 + core, zh * 2 + 1 - core, (1 - zh) * 2 + core, (1 - zh) * 2 + 1 - core, zl * pooled, here]
    at = jnp.stack(places).astype(jnp.int32)

    part = jax.ShapeDtypeStruct((tokens, 3 * mine), BF16)
    parts = (
        part,
        part,
        jax.ShapeDtypeStruct((2, tokens, mine), BF16),
        jax.ShapeDtypeStruct((2, tokens, 2 * mine), BF16),
        jax.ShapeDtypeStruct((8, pooled, 2 * mine), BF16),
    )
    own, near, qz, kvz, copies = pl.pallas_call(
        pack,
        out_shape=parts,
        in_specs=[SMEM] + [ANY] * 5,
        out_specs=(pl.BlockSpec(),) * 5,
        scratch_shapes=[pltpu.VMEM((tokens, width), BF16)] * 3
        + [pltpu.VMEM((pooled, mine), BF16)] * 2
        + [pltpu.SemaphoreType.DMA((5,))],
        cost_estimate=pl.CostEstimate(flops=0, bytes_accessed=3 << 20, transcendentals=0),
        name="pack",
    )(at, q_fresh, k_fresh, v_fresh, k_stale, v_stale)
    line = lax.all_to_all(copies, "zl", split_axis=0, concat_axis=0).reshape(8 * pooled, 2 * mine)
    near = lax.ppermute(near, EVERY, flips(0, 1))
    qz = lax.ppermute(qz, EVERY, flips(1, 0))
    kvz = lax.ppermute(kvz, EVERY, flips(1, 0))
    block = (1, 8 * pooled, 2 * mine)
    planes = pl.pallas_call(
        spread,
        out_shape=jax.ShapeDtypeStruct((16, *block[1:]), BF16),
        grid=(16,),
        in_specs=[pl.BlockSpec(block[1:], lambda i: (0, 0)), ANY, ANY],
        out_specs=pl.BlockSpec(block, lambda i: (i, 0, 0)),
        compiler_params=pltpu.CompilerParams(vmem_limit_bytes=60 << 20),
        cost_estimate=pl.CostEstimate(flops=0, bytes_accessed=3 << 20, transcendentals=0),
        name="spread",
    )(line, near, qz)
    qc = lax.ppermute(qz, EVERY, flips(0, 1))
    kvc = lax.ppermute(kvz, EVERY, flips(0, 1))
    pool = lax.all_to_all(planes, ("y", "x"), split_axis=0, concat_axis=0)
    total_keys = 16 * 8 * pooled + 4 * tokens
    out = pl.pallas_call(
        attend,
        out_shape=jax.ShapeDtypeStruct((4, tokens, mine), BF16),
        in_specs=[SMEM] + [ANY] * 7,
        out_specs=ANY,
        scratch_shapes=[
            pltpu.VMEM((4, tokens, mine), BF16),
            pltpu.VMEM((total_keys, mine), BF16),
            pltpu.VMEM((total_keys, mine), BF16),
            pltpu.VMEM((heads, ROWS, total_keys), F32),
            pltpu.VMEM((4, tokens, mine), BF16),
            pltpu.SemaphoreType.DMA((12,)),
            pltpu.SemaphoreType.DMA((32,)),
            pltpu.SemaphoreType.DMA((4,)),
        ],
        compiler_params=pltpu.CompilerParams(vmem_limit_bytes=60 << 20),
        cost_estimate=pl.CostEstimate(
            flops=4 * 4 * tokens * heads * total_keys * HD,
            bytes_accessed=6 << 20,
            transcendentals=4 * tokens * heads * total_keys,
        ),
        name="attend",
    )(at, own, near, qz, kvz, qc, kvc, pool)
    back = lax.all_to_all(out, ("zh", "core"), split_axis=0, concat_axis=0)
    return back.transpose(1, 0, 2).reshape(tokens, width)


def solution(mesh):
    fine = Mesh(mesh.devices.reshape(SIZES), EVERY)
    whole = P(EVERY, None)
    part = P(("y", "x", "zl"), ("zh", "core"))
    return jax.shard_map(
        local,
        mesh=fine,
        in_specs=(whole, whole, whole, part, part),
        out_specs=whole,
        check_vma=False,
    )
```

```python
import math

import jax
import jax.numpy as jnp
import numpy as np
from jax import lax
from jax.experimental import pallas as pl
from jax.experimental.pallas import tpu as pltpu
from jax.sharding import Mesh
from jax.sharding import PartitionSpec as P

HD = 128
EVERY = ("y", "x", "zl", "zh", "core")
SIZES = (4, 4, 8, 2, 2)
ROWS = 128
SCALE = HD**-0.5 * math.log2(math.e)
NT = (((1,), (1,)), ((), ()))
F32 = jnp.float32
LIMIT = 60 << 20
FRESH_COST = 60 << 30
BF16 = jnp.bfloat16
ANY = pl.BlockSpec(memory_space=pl.ANY)
SMEM = pl.BlockSpec(memory_space=pltpu.SMEM)


def pack(at_ref, qa, ka, va, ksa, vsa, *refs):
    parts, pooled_ref = refs[0:4], refs[4]
    q_ref, k_ref, v_ref, ks_ref, vs_ref, sem = refs[5:]
    loads = zip((ksa, vsa, qa, ka, va), (ks_ref, vs_ref, q_ref, k_ref, v_ref))
    loads = [pltpu.make_async_copy(a, b, sem.at[i]) for i, (a, b) in enumerate(loads)]
    for c in loads:
        c.start()
    mine = ks_ref.shape[1]
    for c in loads[:2]:
        c.wait()
    for j in range(pooled_ref.shape[0]):
        pooled_ref[j, :, 0:mine] = ks_ref[...]
        pooled_ref[j, :, mine : 2 * mine] = vs_ref[...]
    for t, ref in enumerate((q_ref, k_ref, v_ref)):
        loads[2 + t].wait()
        for p, part in enumerate(parts):
            cols = pl.ds(pl.multiple_of(at_ref[p] * mine, HD), mine)
            part[:, t * mine : (t + 1) * mine] = ref[:, cols]


def spread(line_ref, out_ref, here_ref, sem):
    load = pltpu.make_async_copy(line_ref, here_ref, sem.at[0])
    load.start()
    load.wait()
    copies = [pltpu.make_async_copy(here_ref, out_ref.at[j], sem.at[j]) for j in range(out_ref.shape[0])]
    for c in copies:
        c.start()
    for c in copies:
        c.wait()


def attend_fresh(p0, p1, p2, p3, acc_ref, stat_ref, q_ref, keys_ref, values_ref, sem):
    tokens, mine = q_ref.shape[1:]
    loads = []
    for i, ref in enumerate((p0, p1, p2, p3)):
        rows = pl.ds(i * tokens, tokens)
        for t, to in enumerate((q_ref.at[i], keys_ref.at[rows], values_ref.at[rows])):
            loads.append(pltpu.make_async_copy(ref.at[:, t * mine : (t + 1) * mine], to, sem.at[3 * i + t]))
    for c in loads:
        c.start()
    for c in loads:
        c.wait()
    lane = lax.broadcasted_iota(jnp.int32, (tokens, HD), 1)
    heads = mine // HD

    def rows_step(i, carry):
        stat = jnp.zeros((tokens, HD), F32)
        for h in range(heads):
            cs = slice(h * HD, (h + 1) * HD)
            s = lax.dot_general(q_ref[i, :, cs], keys_ref[:, cs], NT, preferred_element_type=F32)
            top = jnp.max(s, axis=1, keepdims=True)
            w = jnp.exp2(s * SCALE - top * SCALE)
            acc_ref[i, :, cs] = jnp.dot(w.astype(BF16), values_ref[:, cs], preferred_element_type=F32)
            stat = jnp.where(lane == 2 * h, top, stat)
            stat = jnp.where(lane == 2 * h + 1, jnp.sum(w, axis=1, keepdims=True), stat)
        stat_ref[i] = stat
        return carry

    lax.fori_loop(0, 4, rows_step, 0)


def attend(at_ref, p0, p1, p2, p3, acc_in, stat_in, pool_ref, out_ref, *scratch):
    q_ref, acc_ref, stat_ref, keys_ref, values_ref, s_ref, res_ref, sem_f, sem_k, sem_o = scratch
    tokens, mine = res_ref.shape[1:]
    heads = mine // HD
    blocks, block = pool_ref.shape[0], pool_ref.shape[1]
    here = at_ref[5]
    loads = []
    for i, ref in enumerate((p0, p1, p2, p3)):
        loads.append(pltpu.make_async_copy(ref.at[:, 0:mine], q_ref.at[i], sem_f.at[i]))
    loads.append(pltpu.make_async_copy(acc_in, acc_ref, sem_f.at[4]))
    loads.append(pltpu.make_async_copy(stat_in, stat_ref, sem_f.at[5]))
    for t, to in enumerate((keys_ref, values_ref)):
        for j in range(blocks):
            src = pool_ref.at[lax.rem(here + j, blocks)]
            rows = pl.ds(j * block, block)
            loads.append(
                pltpu.make_async_copy(src.at[:, t * mine : (t + 1) * mine], to.at[rows], sem_k.at[t * blocks + j])
            )
    for c in loads:
        c.start()
    for c in loads:
        c.wait()
    first = at_ref[4]
    cols = lax.broadcasted_iota(jnp.int32, (ROWS, block), 1)
    own = (cols >= first) & (cols < first + 16)
    chunk = 512
    total_keys = keys_ref.shape[0]

    def rows_step(i, carry):
        for h in range(heads):
            cs = slice(h * HD, (h + 1) * HD)
            q = q_ref[i, :, cs]
            before = stat_ref[i, :, 2 * h : 2 * h + 1]
            top = jnp.broadcast_to(before, (ROWS, HD))
            for c in range(0, total_keys, chunk):
                s = lax.dot_general(q, keys_ref[c : c + chunk, cs], NT, preferred_element_type=F32)
                for d in range(0, chunk, HD):
                    piece = s[:, d : d + HD]
                    if c + d == 0:
                        piece = jnp.where(own, -jnp.inf, piece)
                    s_ref[h, :, c + d : c + d + HD] = piece
                    top = jnp.maximum(top, piece)
            top = jnp.max(top, axis=1, keepdims=True)
            shrink = jnp.exp2((before - top) * SCALE)
            top = top * SCALE
            sums = jnp.zeros((ROWS, HD), F32)
            acc = acc_ref[i, :, cs] * shrink
            for c in range(0, total_keys, chunk):
                w = jnp.exp2(s_ref[h, :, c : c + chunk] * SCALE - top)
                for d in range(0, chunk, HD):
                    sums = sums + w[:, d : d + HD]
                acc = acc + jnp.dot(w.astype(BF16), values_ref[c : c + chunk, cs], preferred_element_type=F32)
            total = jnp.sum(sums, axis=1, keepdims=True) + stat_ref[i, :, 2 * h + 1 : 2 * h + 2] * shrink
            res_ref[i, :, cs] = (acc / total).astype(BF16)
        pltpu.make_async_copy(res_ref.at[i], out_ref.at[at_ref[i]], sem_o.at[i]).start()
        return carry

    lax.fori_loop(0, 4, rows_step, 0)
    for i in range(4):
        pltpu.make_async_copy(res_ref.at[i], out_ref.at[0], sem_o.at[i]).wait()


def flips(zh, core):
    pairs = []
    for i in range(math.prod(SIZES)):
        place = list(np.unravel_index(i, SIZES))
        place[3] ^= zh
        place[4] ^= core
        pairs.append((i, int(np.ravel_multi_index(place, SIZES))))
    return pairs


def local(q_fresh, k_fresh, v_fresh, k_stale, v_stale):
    tokens, width = q_fresh.shape
    pooled, mine = k_stale.shape
    heads = mine // HD
    zh, core = lax.axis_index("zh"), lax.axis_index("core")
    zl, here = lax.axis_index("zl"), lax.axis_index("y") * 4 + lax.axis_index("x")
    places = [zh * 2 + core, zh * 2 + 1 - core, (1 - zh) * 2 + core, (1 - zh) * 2 + 1 - core, zl * pooled, here]
    at = jnp.stack(places).astype(jnp.int32)

    dma = pltpu.SemaphoreType.DMA
    part = jax.ShapeDtypeStruct((tokens, 3 * mine), BF16)
    own, near, same, other, copies = pl.pallas_call(
        pack,
        out_shape=(part,) * 4 + (jax.ShapeDtypeStruct((8, pooled, 2 * mine), BF16),),
        in_specs=[SMEM] + [ANY] * 5,
        out_specs=(pl.BlockSpec(),) * 5,
        scratch_shapes=[pltpu.VMEM((tokens, width), BF16)] * 3 + [pltpu.VMEM((pooled, mine), BF16)] * 2 + [dma((5,))],
        compiler_params=pltpu.CompilerParams(vmem_limit_bytes=LIMIT),
        cost_estimate=pl.CostEstimate(flops=0, bytes_accessed=3 << 20, transcendentals=0),
        name="pack",
    )(at, q_fresh, k_fresh, v_fresh, k_stale, v_stale)
    near = lax.ppermute(near, EVERY, flips(0, 1))
    same = lax.ppermute(same, EVERY, flips(1, 0))
    other = lax.ppermute(other, EVERY, flips(1, 1))
    line = lax.all_to_all(copies, "zl", split_axis=0, concat_axis=0).reshape(8 * pooled, 2 * mine)
    planes = pl.pallas_call(
        spread,
        out_shape=jax.ShapeDtypeStruct((16, 8 * pooled, 2 * mine), BF16),
        in_specs=[ANY],
        out_specs=ANY,
        scratch_shapes=[pltpu.VMEM((8 * pooled, 2 * mine), BF16), dma((16,))],
        compiler_params=pltpu.CompilerParams(vmem_limit_bytes=LIMIT),
        cost_estimate=pl.CostEstimate(flops=0, bytes_accessed=3 << 20, transcendentals=0),
        name="spread",
    )(line)
    pool = lax.all_to_all(planes, ("y", "x"), split_axis=0, concat_axis=0)

    fresh = 4 * tokens
    block = (4, tokens, mine)
    acc, stat = pl.pallas_call(
        attend_fresh,
        out_shape=(jax.ShapeDtypeStruct(block, F32), jax.ShapeDtypeStruct((4, tokens, HD), F32)),
        in_specs=[ANY] * 4,
        out_specs=(pl.BlockSpec(),) * 2,
        scratch_shapes=[pltpu.VMEM(block, BF16)] + [pltpu.VMEM((fresh, mine), BF16)] * 2 + [dma((12,))],
        compiler_params=pltpu.CompilerParams(vmem_limit_bytes=LIMIT),
        cost_estimate=pl.CostEstimate(flops=FRESH_COST, bytes_accessed=3 << 20, transcendentals=0),
        name="attend_fresh",
    )(own, near, same, other)
    total_keys = 16 * 8 * pooled
    out = pl.pallas_call(
        attend,
        out_shape=jax.ShapeDtypeStruct(block, BF16),
        in_specs=[SMEM] + [ANY] * 7,
        out_specs=ANY,
        scratch_shapes=[
            pltpu.VMEM(block, BF16),
            pltpu.VMEM(block, F32),
            pltpu.VMEM((4, tokens, HD), F32),
            pltpu.VMEM((total_keys, mine), BF16),
            pltpu.VMEM((total_keys, mine), BF16),
            pltpu.VMEM((heads, ROWS, total_keys), F32),
            pltpu.VMEM(block, BF16),
            dma((6,)),
            dma((32,)),
            dma((4,)),
        ],
        compiler_params=pltpu.CompilerParams(vmem_limit_bytes=LIMIT),
        cost_estimate=pl.CostEstimate(
            flops=4 * fresh * heads * total_keys * HD,
            bytes_accessed=6 << 20,
            transcendentals=fresh * heads * total_keys,
        ),
        name="attend",
    )(at, own, near, same, other, acc, stat, pool)
    back = lax.all_to_all(out, ("zh", "core"), split_axis=0, concat_axis=0)
    return back.transpose(1, 0, 2).reshape(tokens, width)


def solution(mesh):
    fine = Mesh(mesh.devices.reshape(SIZES), EVERY)
    whole = P(EVERY, None)
    part = P(("y", "x", "zl"), ("zh", "core"))
    return jax.shard_map(
        local,
        mesh=fine,
        in_specs=(whole, whole, whole, part, part),
        out_specs=whole,
        check_vma=False,
    )
```

```python
import math

import jax
import jax.numpy as jnp
import numpy as np
from jax import lax
from jax.experimental import pallas as pl
from jax.experimental.pallas import tpu as pltpu
from jax.sharding import Mesh
from jax.sharding import PartitionSpec as P

HD = 128
EVERY = ("y", "x", "zl", "zh", "core")
SIZES = (4, 4, 8, 2, 2)
SCALE = HD**-0.5 * math.log2(math.e)
NT = (((1,), (1,)), ((), ()))
F32 = jnp.float32
LIMIT = 60 << 20
SPREAD_LIMIT = 48 << 20
ATTEND_LIMIT = 48 << 20
FRESH_COST = 60 << 30
BF16 = jnp.bfloat16
ANY = pl.BlockSpec(memory_space=pl.ANY)
VMEM = pl.BlockSpec(memory_space=pltpu.VMEM)


def peers():
    zh, core = lax.axis_index("zh"), lax.axis_index("core")
    return [a * 2 + b for a in (zh, 1 - zh) for b in (core, 1 - core)]


def pack(qa, ka, va, ksa, vsa, *refs):
    parts, pooled_ref = refs[0:4], refs[4]
    q_ref, k_ref, v_ref, ks_ref, vs_ref, sem = refs[5:]
    loads = zip((ksa, vsa, qa, ka, va), (ks_ref, vs_ref, q_ref, k_ref, v_ref))
    loads = [pltpu.make_async_copy(a, b, sem.at[i]) for i, (a, b) in enumerate(loads)]
    for c in loads:
        c.start()
    mine = ks_ref.shape[1]
    for c in loads[:2]:
        c.wait()
    for j in range(pooled_ref.shape[0]):
        pooled_ref[j, :, 0:mine] = ks_ref[...]
        pooled_ref[j, :, mine : 2 * mine] = vs_ref[...]
    places = peers()
    for t, ref in enumerate((q_ref, k_ref, v_ref)):
        loads[2 + t].wait()
        for p, part in enumerate(parts):
            cols = pl.ds(pl.multiple_of(places[p] * mine, HD), mine)
            part[:, t * mine : (t + 1) * mine] = ref[:, cols]


def spread(line_ref, near_ref, out_ref, same_ref, sem):
    copies = [pltpu.make_async_copy(line_ref, out_ref.at[j], sem.at[j]) for j in range(out_ref.shape[0])]
    for c in copies:
        c.start()
    for c in copies:
        c.wait()


def attend_fresh(p0, p1, p2, p3, carry_ref, q_ref, keys_ref, values_ref, sem):
    tokens, mine = q_ref.shape[1:]
    loads = []
    for i, ref in enumerate((p0, p1, p2, p3)):
        rows = pl.ds(i * tokens, tokens)
        for t, to in enumerate((q_ref.at[i], keys_ref.at[rows], values_ref.at[rows])):
            loads.append(pltpu.make_async_copy(ref.at[:, t * mine : (t + 1) * mine], to, sem.at[3 * i + t]))
    for c in loads:
        c.start()
    for c in loads:
        c.wait()
    lane = lax.broadcasted_iota(jnp.int32, (tokens, HD), 1)
    heads = mine // HD

    def rows_step(i, carry):
        stat = jnp.zeros((tokens, HD), F32)
        rows = pl.ds(pl.multiple_of(i * tokens, tokens), tokens)
        for h in range(heads):
            cs = slice(h * HD, (h + 1) * HD)
            q = q_ref[i, :, cs]
            s = lax.dot_general(q, keys_ref[:, cs], NT, preferred_element_type=F32)
            top = jnp.max(s, axis=1, keepdims=True)
            w = jnp.exp2(s * SCALE - top * SCALE)
            carry_ref[rows, cs] = q.astype(F32)
            carry_ref[rows, mine + h * HD : mine + (h + 1) * HD] = jnp.dot(
                w.astype(BF16), values_ref[:, cs], preferred_element_type=F32
            )
            stat = jnp.where(lane == 2 * h, top, stat)
            stat = jnp.where(lane == 2 * h + 1, jnp.sum(w, axis=1, keepdims=True), stat)
        carry_ref[rows, 2 * mine :] = stat
        return carry

    lax.fori_loop(0, 4, rows_step, 0)


def attend(carry_ref, pool_ref, out_ref, s_ref):
    tokens, mine = out_ref.shape[1:]
    heads = mine // HD
    blocks, block = pool_ref.shape[0], pool_ref.shape[1]
    stale = blocks * block
    here = lax.axis_index("y") * 4 + lax.axis_index("x")
    first = here * block + lax.axis_index("zl") * (block // 8)
    col = lax.broadcasted_iota(jnp.int32, (tokens, block), 1)
    places = peers()
    steps = [(h, i) for i in range(4) for h in range(heads)]
    tops = {}

    def own(b):
        return (col >= first - b * block) & (col < first - b * block + block // 8)

    def scores(n):
        h, i = steps[n]
        rows = slice(i * tokens, (i + 1) * tokens)
        cs = slice(h * HD, (h + 1) * HD)
        q = carry_ref[rows, cs].astype(BF16)
        before = carry_ref[rows, 2 * mine + 2 * h : 2 * mine + 2 * h + 1]
        top = jnp.broadcast_to(before, (tokens, HD))
        for b in range(0, blocks, 4):
            keys = pool_ref[b : b + 4, :, cs].reshape(4 * block, HD)
            s = lax.dot_general(q, keys, NT, preferred_element_type=F32)
            for d in range(4):
                piece = jnp.where(own(b + d), -jnp.inf, s[:, d * block : (d + 1) * block])
                s_ref[n % 2, :, (b + d) * block : (b + d + 1) * block] = piece
                top = jnp.maximum(top, piece)
        tops[n] = (before, jnp.max(top, axis=1, keepdims=True))

    def weigh(n):
        h, i = steps[n]
        rows = slice(i * tokens, (i + 1) * tokens)
        cs = slice(mine + h * HD, mine + (h + 1) * HD)
        before, top = tops.pop(n)
        shrink = jnp.exp2((before - top) * SCALE)
        top = top * SCALE
        sums = jnp.zeros((tokens, HD), F32)
        acc = carry_ref[rows, cs] * shrink
        for b in range(0, blocks, 4):
            w = jnp.exp2(s_ref[n % 2, :, b * block : (b + 4) * block] * SCALE - top)
            for d in range(4):
                sums = sums + w[:, d * block : (d + 1) * block]
            values = pool_ref[b : b + 4, :, cs].reshape(4 * block, HD)
            acc = acc + jnp.dot(w.astype(BF16), values, preferred_element_type=F32)
        total = carry_ref[rows, 2 * mine + 2 * h + 1 : 2 * mine + 2 * h + 2] * shrink
        total = total + jnp.sum(sums, axis=1, keepdims=True)
        out_ref[places[i], :, h * HD : (h + 1) * HD] = (acc / total).astype(BF16)

    scores(0)
    for n in range(len(steps)):
        if n + 1 < len(steps):
            scores(n + 1)
        weigh(n)


def flips(zh, core):
    pairs = []
    for i in range(math.prod(SIZES)):
        place = list(np.unravel_index(i, SIZES))
        place[3] ^= zh
        place[4] ^= core
        pairs.append((i, int(np.ravel_multi_index(place, SIZES))))
    return pairs


def local(q_fresh, k_fresh, v_fresh, k_stale, v_stale):
    tokens, width = q_fresh.shape
    pooled, mine = k_stale.shape
    heads = mine // HD
    dma = pltpu.SemaphoreType.DMA
    part = jax.ShapeDtypeStruct((tokens, 3 * mine), BF16)
    own, near, same, other, copies = pl.pallas_call(
        pack,
        out_shape=(part,) * 4 + (jax.ShapeDtypeStruct((8, pooled, 2 * mine), BF16),),
        in_specs=[ANY] * 5,
        out_specs=(pl.BlockSpec(),) * 5,
        scratch_shapes=[pltpu.VMEM((tokens, width), BF16)] * 3 + [pltpu.VMEM((pooled, mine), BF16)] * 2 + [dma((5,))],
        compiler_params=pltpu.CompilerParams(vmem_limit_bytes=LIMIT),
        cost_estimate=pl.CostEstimate(flops=0, bytes_accessed=3 << 20, transcendentals=0),
        name="pack",
    )(q_fresh, k_fresh, v_fresh, k_stale, v_stale)
    same = lax.ppermute(same, EVERY, flips(1, 0))
    other = lax.ppermute(other, EVERY, flips(1, 1))
    line = lax.all_to_all(copies, "zl", split_axis=0, concat_axis=0).reshape(8 * pooled, 2 * mine)
    planes, near = pl.pallas_call(
        spread,
        out_shape=(jax.ShapeDtypeStruct((16, 8 * pooled, 2 * mine), BF16), part),
        in_specs=[VMEM, ANY],
        out_specs=(ANY, ANY),
        scratch_shapes=[dma((16,))],
        input_output_aliases={1: 1},
        compiler_params=pltpu.CompilerParams(vmem_limit_bytes=SPREAD_LIMIT),
        cost_estimate=pl.CostEstimate(flops=0, bytes_accessed=3 << 20, transcendentals=0),
        name="spread",
    )(line, near)
    near = lax.ppermute(near, EVERY, flips(0, 1))
    pool = lax.all_to_all(planes, ("y", "x"), split_axis=0, concat_axis=0)

    fresh = 4 * tokens
    carry = jax.ShapeDtypeStruct((fresh, 2 * mine + HD), F32)
    carry = pl.pallas_call(
        attend_fresh,
        out_shape=carry,
        in_specs=[ANY] * 4,
        scratch_shapes=[pltpu.VMEM((4, tokens, mine), BF16)] + [pltpu.VMEM((fresh, mine), BF16)] * 2 + [dma((12,))],
        compiler_params=pltpu.CompilerParams(vmem_limit_bytes=LIMIT),
        cost_estimate=pl.CostEstimate(flops=FRESH_COST, bytes_accessed=3 << 20, transcendentals=0),
        name="attend_fresh",
    )(own, near, same, other)
    total_keys = 16 * 8 * pooled
    out = pl.pallas_call(
        attend,
        out_shape=jax.ShapeDtypeStruct((4, tokens, mine), BF16),
        in_specs=[VMEM, VMEM],
        out_specs=VMEM,
        scratch_shapes=[pltpu.VMEM((2, tokens, total_keys), F32)],
        compiler_params=pltpu.CompilerParams(vmem_limit_bytes=ATTEND_LIMIT),
        cost_estimate=pl.CostEstimate(
            flops=4 * fresh * heads * total_keys * HD,
            bytes_accessed=6 << 20,
            transcendentals=fresh * heads * total_keys,
        ),
        name="attend",
    )(carry, pool)
    back = lax.all_to_all(out, ("zh", "core"), split_axis=0, concat_axis=0)
    return back.transpose(1, 0, 2).reshape(tokens, width)


def solution(mesh):
    fine = Mesh(mesh.devices.reshape(SIZES), EVERY)
    whole = P(EVERY, None)
    part = P(("y", "x", "zl"), ("zh", "core"))
    return jax.shard_map(
        local,
        mesh=fine,
        in_specs=(whole, whole, whole, part, part),
        out_specs=whole,
        check_vma=False,
    )
```

```python
import math

import jax
import jax.numpy as jnp
import numpy as np
from jax import lax
from jax.experimental import pallas as pl
from jax.experimental.pallas import tpu as pltpu
from jax.sharding import Mesh
from jax.sharding import PartitionSpec as P

HD = 128
EVERY = ("y", "x", "zl", "zh", "core")
SIZES = (4, 4, 8, 2, 2)
SCALE = HD**-0.5 * math.log2(math.e)
NT = (((1,), (1,)), ((), ()))
F32 = jnp.float32
LIMIT = 60 << 20
SPREAD_LIMIT = 48 << 20
ATTEND_LIMIT = 48 << 20
FRESH_COST = 60 << 30
BF16 = jnp.bfloat16
ANY = pl.BlockSpec(memory_space=pl.ANY)
VMEM = pl.BlockSpec(memory_space=pltpu.VMEM)


def peers():
    zh, core = lax.axis_index("zh"), lax.axis_index("core")
    return [a * 2 + b for a in (zh, 1 - zh) for b in (core, 1 - core)]


def pack(qa, ka, va, ksa, vsa, *refs):
    parts, pooled_ref = refs[0:4], refs[4]
    q_ref, k_ref, v_ref, ks_ref, vs_ref, sem = refs[5:]
    loads = zip((ksa, vsa, qa, ka, va), (ks_ref, vs_ref, q_ref, k_ref, v_ref))
    loads = [pltpu.make_async_copy(a, b, sem.at[i]) for i, (a, b) in enumerate(loads)]
    for c in loads:
        c.start()
    mine = ks_ref.shape[1]
    for c in loads[:2]:
        c.wait()
    for j in range(pooled_ref.shape[0]):
        pooled_ref[j, :, 0:mine] = ks_ref[...]
        pooled_ref[j, :, mine : 2 * mine] = vs_ref[...]
    places = peers()
    for t, ref in enumerate((q_ref, k_ref, v_ref)):
        loads[2 + t].wait()
        for p, part in enumerate(parts):
            cols = pl.ds(pl.multiple_of(places[p] * mine, HD), mine)
            part[:, t * mine : (t + 1) * mine] = ref[:, cols]


def spread(line_ref, out_ref, sem):
    copies = [pltpu.make_async_copy(line_ref, out_ref.at[j], sem.at[j]) for j in range(out_ref.shape[0])]
    for c in copies:
        c.start()
    for c in copies:
        c.wait()


def attend_fresh(p0, p1, p2, p3, carry_ref, q_ref, keys_ref, values_ref, sem):
    tokens, mine = q_ref.shape[1:]
    loads = []
    for i, ref in enumerate((p0, p1, p2, p3)):
        rows = pl.ds(i * tokens, tokens)
        for t, to in enumerate((q_ref.at[i], keys_ref.at[rows], values_ref.at[rows])):
            loads.append(pltpu.make_async_copy(ref.at[:, t * mine : (t + 1) * mine], to, sem.at[3 * i + t]))
    for c in loads:
        c.start()
    for c in loads:
        c.wait()
    lane = lax.broadcasted_iota(jnp.int32, (tokens, HD), 1)
    heads = mine // HD

    def rows_step(i, carry):
        stat = jnp.zeros((tokens, HD), F32)
        rows = pl.ds(pl.multiple_of(i * tokens, tokens), tokens)
        for h in range(heads):
            cs = slice(h * HD, (h + 1) * HD)
            q = q_ref[i, :, cs]
            s = lax.dot_general(q, keys_ref[:, cs], NT, preferred_element_type=F32)
            top = jnp.max(s, axis=1, keepdims=True)
            w = jnp.exp2(s * SCALE - top * SCALE)
            carry_ref[rows, cs] = q.astype(F32)
            carry_ref[rows, mine + h * HD : mine + (h + 1) * HD] = jnp.dot(
                w.astype(BF16), values_ref[:, cs], preferred_element_type=F32
            )
            stat = jnp.where(lane == 2 * h, top, stat)
            stat = jnp.where(lane == 2 * h + 1, jnp.sum(w, axis=1, keepdims=True), stat)
        carry_ref[rows, 2 * mine :] = stat
        return carry

    lax.fori_loop(0, 4, rows_step, 0)


def attend(carry_ref, pool_ref, out_ref, s_ref):
    tokens, mine = out_ref.shape[1:]
    heads = mine // HD
    blocks, block = pool_ref.shape[0], pool_ref.shape[1]
    stale = blocks * block
    here = lax.axis_index("y") * 4 + lax.axis_index("x")
    first = here * block + lax.axis_index("zl") * (block // 8)
    col = lax.broadcasted_iota(jnp.int32, (tokens, block), 1)
    places = peers()
    steps = [(h, i) for i in range(4) for h in range(heads)]
    tops = {}

    def own(b):
        return (col >= first - b * block) & (col < first - b * block + block // 8)

    def scores(n):
        h, i = steps[n]
        rows = slice(i * tokens, (i + 1) * tokens)
        cs = slice(h * HD, (h + 1) * HD)
        q = carry_ref[rows, cs].astype(BF16)
        before = carry_ref[rows, 2 * mine + 2 * h : 2 * mine + 2 * h + 1]
        top = jnp.broadcast_to(before, (tokens, HD))
        for b in range(0, blocks, 4):
            keys = pool_ref[b : b + 4, :, cs].reshape(4 * block, HD)
            s = lax.dot_general(q, keys, NT, preferred_element_type=F32)
            for d in range(4):
                piece = jnp.where(own(b + d), -jnp.inf, s[:, d * block : (d + 1) * block])
                s_ref[n % 2, :, (b + d) * block : (b + d + 1) * block] = piece
                top = jnp.maximum(top, piece)
        tops[n] = (before, jnp.max(top, axis=1, keepdims=True))

    def weigh(n):
        h, i = steps[n]
        rows = slice(i * tokens, (i + 1) * tokens)
        cs = slice(mine + h * HD, mine + (h + 1) * HD)
        before, top = tops.pop(n)
        shrink = jnp.exp2((before - top) * SCALE)
        top = top * SCALE
        sums = jnp.zeros((tokens, HD), F32)
        acc = carry_ref[rows, cs] * shrink
        for b in range(0, blocks, 4):
            w = jnp.exp2(s_ref[n % 2, :, b * block : (b + 4) * block] * SCALE - top)
            for d in range(4):
                sums = sums + w[:, d * block : (d + 1) * block]
            values = pool_ref[b : b + 4, :, cs].reshape(4 * block, HD)
            acc = acc + jnp.dot(w.astype(BF16), values, preferred_element_type=F32)
        total = carry_ref[rows, 2 * mine + 2 * h + 1 : 2 * mine + 2 * h + 2] * shrink
        total = total + jnp.sum(sums, axis=1, keepdims=True)
        out_ref[places[i], :, h * HD : (h + 1) * HD] = (acc / total).astype(BF16)

    scores(0)
    for n in range(len(steps)):
        if n + 1 < len(steps):
            scores(n + 1)
        weigh(n)


def flips(zh, core):
    pairs = []
    for i in range(math.prod(SIZES)):
        place = list(np.unravel_index(i, SIZES))
        place[3] ^= zh
        place[4] ^= core
        pairs.append((i, int(np.ravel_multi_index(place, SIZES))))
    return pairs


def local(q_fresh, k_fresh, v_fresh, k_stale, v_stale):
    tokens, width = q_fresh.shape
    pooled, mine = k_stale.shape
    heads = mine // HD
    dma = pltpu.SemaphoreType.DMA
    part = jax.ShapeDtypeStruct((tokens, 3 * mine), BF16)
    own, near, same, other, copies = pl.pallas_call(
        pack,
        out_shape=(part,) * 4 + (jax.ShapeDtypeStruct((8, pooled, 2 * mine), BF16),),
        in_specs=[ANY] * 5,
        out_specs=(pl.BlockSpec(),) * 5,
        scratch_shapes=[pltpu.VMEM((tokens, width), BF16)] * 3 + [pltpu.VMEM((pooled, mine), BF16)] * 2 + [dma((5,))],
        compiler_params=pltpu.CompilerParams(vmem_limit_bytes=LIMIT),
        cost_estimate=pl.CostEstimate(flops=0, bytes_accessed=3 << 20, transcendentals=0),
        name="pack",
    )(q_fresh, k_fresh, v_fresh, k_stale, v_stale)
    near = lax.ppermute(near, EVERY, flips(0, 1))
    same = lax.ppermute(same, EVERY, flips(1, 0))
    other = lax.ppermute(other, EVERY, flips(1, 1))
    line = lax.all_to_all(copies, "zl", split_axis=0, concat_axis=0).reshape(8 * pooled, 2 * mine)
    planes = pl.pallas_call(
        spread,
        out_shape=jax.ShapeDtypeStruct((16, 8 * pooled, 2 * mine), BF16),
        in_specs=[VMEM],
        out_specs=ANY,
        scratch_shapes=[dma((16,))],
        compiler_params=pltpu.CompilerParams(vmem_limit_bytes=SPREAD_LIMIT),
        cost_estimate=pl.CostEstimate(flops=0, bytes_accessed=3 << 20, transcendentals=0),
        name="spread",
    )(line)
    pool = lax.all_to_all(planes, ("y", "x"), split_axis=0, concat_axis=0)

    fresh = 4 * tokens
    carry = jax.ShapeDtypeStruct((fresh, 2 * mine + HD), F32)
    carry = pl.pallas_call(
        attend_fresh,
        out_shape=carry,
        in_specs=[ANY] * 4,
        scratch_shapes=[pltpu.VMEM((4, tokens, mine), BF16)] + [pltpu.VMEM((fresh, mine), BF16)] * 2 + [dma((12,))],
        compiler_params=pltpu.CompilerParams(vmem_limit_bytes=LIMIT),
        cost_estimate=pl.CostEstimate(flops=FRESH_COST, bytes_accessed=3 << 20, transcendentals=0),
        name="attend_fresh",
    )(own, near, same, other)
    total_keys = 16 * 8 * pooled
    out = pl.pallas_call(
        attend,
        out_shape=jax.ShapeDtypeStruct((4, tokens, mine), BF16),
        in_specs=[VMEM, VMEM],
        out_specs=VMEM,
        scratch_shapes=[pltpu.VMEM((2, tokens, total_keys), F32)],
        compiler_params=pltpu.CompilerParams(vmem_limit_bytes=ATTEND_LIMIT),
        cost_estimate=pl.CostEstimate(
            flops=4 * fresh * heads * total_keys * HD,
            bytes_accessed=6 << 20,
            transcendentals=fresh * heads * total_keys,
        ),
        name="attend",
    )(carry, pool)
    back = lax.all_to_all(out, ("zh", "core"), split_axis=0, concat_axis=0)
    return back.transpose(1, 0, 2).reshape(tokens, width)


def solution(mesh):
    fine = Mesh(mesh.devices.reshape(SIZES), EVERY)
    whole = P(EVERY, None)
    part = P(("y", "x", "zl"), ("zh", "core"))
    return jax.shard_map(
        local,
        mesh=fine,
        in_specs=(whole, whole, whole, part, part),
        out_specs=whole,
        check_vma=False,
    )
```

```python
import math

import jax
import jax.numpy as jnp
import numpy as np
from jax import lax
from jax.experimental import pallas as pl
from jax.experimental.pallas import tpu as pltpu
from jax.sharding import Mesh
from jax.sharding import PartitionSpec as P

HD = 128
EVERY = ("y", "x", "zl", "zh", "core")
SIZES = (4, 4, 8, 2, 2)
SCALE = HD**-0.5 * math.log2(math.e)
NT = (((1,), (1,)), ((), ()))
F32 = jnp.float32
LIMIT = 60 << 20
SPREAD_LIMIT = 55 << 20
ATTEND_LIMIT = 48 << 20
FRESH_COST = 1 << 30
ARRIVE_COST = 60 << 30
BF16 = jnp.bfloat16
ANY = pl.BlockSpec(memory_space=pl.ANY)
VMEM = pl.BlockSpec(memory_space=pltpu.VMEM)


def peers():
    zh, core = lax.axis_index("zh"), lax.axis_index("core")
    return [a * 2 + b for a in (zh, 1 - zh) for b in (core, 1 - core)]


def pack(qa, ka, va, ksa, vsa, *refs):
    parts, pooled_ref = refs[0:4], refs[4]
    q_ref, k_ref, v_ref, ks_ref, vs_ref, sem = refs[5:]
    loads = zip((ksa, vsa, qa, ka, va), (ks_ref, vs_ref, q_ref, k_ref, v_ref))
    loads = [pltpu.make_async_copy(a, b, sem.at[i]) for i, (a, b) in enumerate(loads)]
    for c in loads:
        c.start()
    mine = ks_ref.shape[1]
    for c in loads[:2]:
        c.wait()
    for j in range(pooled_ref.shape[0]):
        pooled_ref[j, :, 0:mine] = ks_ref[...]
        pooled_ref[j, :, mine : 2 * mine] = vs_ref[...]
    places = peers()
    for t, ref in enumerate((q_ref, k_ref, v_ref)):
        loads[2 + t].wait()
        for p, part in enumerate(parts):
            cols = pl.ds(pl.multiple_of(places[p] * mine, HD), mine)
            part[:, t * mine : (t + 1) * mine] = ref[:, cols]


def spread(line_ref, other_ref, out_ref, same_ref, sem):
    copies = [pltpu.make_async_copy(line_ref, out_ref.at[j], sem.at[j]) for j in range(out_ref.shape[0])]
    for c in copies:
        c.start()
    for c in copies:
        c.wait()


def arrive(near_ref, same_ref, near_out, same_out):
    pass


def attend_fresh(p0, p1, p2, p3, carry_ref, q_ref, keys_ref, values_ref, sem):
    tokens, mine = q_ref.shape[1:]
    loads = []
    for i, ref in enumerate((p0, p1, p2, p3)):
        rows = pl.ds(i * tokens, tokens)
        for t, to in enumerate((q_ref.at[i], keys_ref.at[rows], values_ref.at[rows])):
            loads.append(pltpu.make_async_copy(ref.at[:, t * mine : (t + 1) * mine], to, sem.at[3 * i + t]))
    for c in loads:
        c.start()
    for c in loads:
        c.wait()
    lane = lax.broadcasted_iota(jnp.int32, (tokens, HD), 1)
    heads = mine // HD

    def rows_step(i, carry):
        stat = jnp.zeros((tokens, HD), F32)
        rows = pl.ds(pl.multiple_of(i * tokens, tokens), tokens)
        for h in range(heads):
            cs = slice(h * HD, (h + 1) * HD)
            q = q_ref[i, :, cs]
            s = lax.dot_general(q, keys_ref[:, cs], NT, preferred_element_type=F32)
            top = jnp.max(s, axis=1, keepdims=True)
            w = jnp.exp2(s * SCALE - top * SCALE)
            carry_ref[rows, cs] = q.astype(F32)
            carry_ref[rows, mine + h * HD : mine + (h + 1) * HD] = jnp.dot(
                w.astype(BF16), values_ref[:, cs], preferred_element_type=F32
            )
            stat = jnp.where(lane == 2 * h, top, stat)
            stat = jnp.where(lane == 2 * h + 1, jnp.sum(w, axis=1, keepdims=True), stat)
        carry_ref[rows, 2 * mine :] = stat
        return carry

    lax.fori_loop(0, 4, rows_step, 0)


def attend(carry_ref, pool_ref, out_ref, s_ref):
    tokens, mine = out_ref.shape[1:]
    heads = mine // HD
    blocks, block = pool_ref.shape[0], pool_ref.shape[1]
    stale = blocks * block
    here = lax.axis_index("y") * 4 + lax.axis_index("x")
    first = here * block + lax.axis_index("zl") * (block // 8)
    col = lax.broadcasted_iota(jnp.int32, (tokens, block), 1)
    places = peers()
    steps = [(h, i) for i in range(4) for h in range(heads)]
    tops = {}

    def own(b):
        return (col >= first - b * block) & (col < first - b * block + block // 8)

    def scores(n):
        h, i = steps[n]
        rows = slice(i * tokens, (i + 1) * tokens)
        cs = slice(h * HD, (h + 1) * HD)
        q = carry_ref[rows, cs].astype(BF16)
        before = carry_ref[rows, 2 * mine + 2 * h : 2 * mine + 2 * h + 1]
        top = jnp.broadcast_to(before, (tokens, HD))
        for b in range(0, blocks, 4):
            keys = pool_ref[b : b + 4, :, cs].reshape(4 * block, HD)
            s = lax.dot_general(q, keys, NT, preferred_element_type=F32)
            for d in range(4):
                piece = jnp.where(own(b + d), -jnp.inf, s[:, d * block : (d + 1) * block])
                s_ref[n % 2, :, (b + d) * block : (b + d + 1) * block] = piece
                top = jnp.maximum(top, piece)
        tops[n] = (before, jnp.max(top, axis=1, keepdims=True))

    def weigh(n):
        h, i = steps[n]
        rows = slice(i * tokens, (i + 1) * tokens)
        cs = slice(mine + h * HD, mine + (h + 1) * HD)
        before, top = tops.pop(n)
        shrink = jnp.exp2((before - top) * SCALE)
        top = top * SCALE
        sums = jnp.zeros((tokens, HD), F32)
        acc = carry_ref[rows, cs] * shrink
        for b in range(0, blocks, 4):
            w = jnp.exp2(s_ref[n % 2, :, b * block : (b + 4) * block] * SCALE - top)
            for d in range(4):
                sums = sums + w[:, d * block : (d + 1) * block]
            values = pool_ref[b : b + 4, :, cs].reshape(4 * block, HD)
            acc = acc + jnp.dot(w.astype(BF16), values, preferred_element_type=F32)
        total = carry_ref[rows, 2 * mine + 2 * h + 1 : 2 * mine + 2 * h + 2] * shrink
        total = total + jnp.sum(sums, axis=1, keepdims=True)
        out_ref[places[i], :, h * HD : (h + 1) * HD] = (acc / total).astype(BF16)

    scores(0)
    for n in range(len(steps)):
        if n + 1 < len(steps):
            scores(n + 1)
        weigh(n)


def flips(zh, core):
    pairs = []
    for i in range(math.prod(SIZES)):
        place = list(np.unravel_index(i, SIZES))
        place[3] ^= zh
        place[4] ^= core
        pairs.append((i, int(np.ravel_multi_index(place, SIZES))))
    return pairs


def local(q_fresh, k_fresh, v_fresh, k_stale, v_stale):
    tokens, width = q_fresh.shape
    pooled, mine = k_stale.shape
    heads = mine // HD
    dma = pltpu.SemaphoreType.DMA
    part = jax.ShapeDtypeStruct((tokens, 3 * mine), BF16)
    own, near, same, other, copies = pl.pallas_call(
        pack,
        out_shape=(part,) * 4 + (jax.ShapeDtypeStruct((8, pooled, 2 * mine), BF16),),
        in_specs=[ANY] * 5,
        out_specs=(pl.BlockSpec(),) * 5,
        scratch_shapes=[pltpu.VMEM((tokens, width), BF16)] * 3 + [pltpu.VMEM((pooled, mine), BF16)] * 2 + [dma((5,))],
        compiler_params=pltpu.CompilerParams(vmem_limit_bytes=LIMIT),
        cost_estimate=pl.CostEstimate(flops=0, bytes_accessed=3 << 20, transcendentals=0),
        name="pack",
    )(q_fresh, k_fresh, v_fresh, k_stale, v_stale)
    near = lax.ppermute(near, EVERY, flips(0, 1))
    same = lax.ppermute(same, EVERY, flips(1, 0))
    line = lax.all_to_all(copies, "zl", split_axis=0, concat_axis=0).reshape(8 * pooled, 2 * mine)
    planes, other = pl.pallas_call(
        spread,
        out_shape=(jax.ShapeDtypeStruct((16, 8 * pooled, 2 * mine), BF16), part),
        in_specs=[VMEM, ANY],
        out_specs=(ANY, ANY),
        scratch_shapes=[dma((16,))],
        input_output_aliases={1: 1},
        compiler_params=pltpu.CompilerParams(vmem_limit_bytes=SPREAD_LIMIT),
        cost_estimate=pl.CostEstimate(flops=0, bytes_accessed=3 << 20, transcendentals=0),
        name="spread",
    )(line, other)
    other = lax.ppermute(other, EVERY, flips(1, 1))
    near, same = pl.pallas_call(
        arrive,
        out_shape=(part, part),
        in_specs=[ANY, ANY],
        out_specs=(ANY, ANY),
        input_output_aliases={0: 0, 1: 1},
        compiler_params=pltpu.CompilerParams(vmem_limit_bytes=LIMIT),
        cost_estimate=pl.CostEstimate(flops=ARRIVE_COST, bytes_accessed=0, transcendentals=0),
        name="arrive",
    )(near, same)
    pool = lax.all_to_all(planes, ("y", "x"), split_axis=0, concat_axis=0)

    fresh = 4 * tokens
    carry = jax.ShapeDtypeStruct((fresh, 2 * mine + HD), F32)
    carry = pl.pallas_call(
        attend_fresh,
        out_shape=carry,
        in_specs=[ANY] * 4,
        scratch_shapes=[pltpu.VMEM((4, tokens, mine), BF16)] + [pltpu.VMEM((fresh, mine), BF16)] * 2 + [dma((12,))],
        compiler_params=pltpu.CompilerParams(vmem_limit_bytes=LIMIT),
        cost_estimate=pl.CostEstimate(flops=FRESH_COST, bytes_accessed=3 << 20, transcendentals=0),
        name="attend_fresh",
    )(own, near, same, other)
    total_keys = 16 * 8 * pooled
    out = pl.pallas_call(
        attend,
        out_shape=jax.ShapeDtypeStruct((4, tokens, mine), BF16),
        in_specs=[VMEM, VMEM],
        out_specs=VMEM,
        scratch_shapes=[pltpu.VMEM((2, tokens, total_keys), F32)],
        compiler_params=pltpu.CompilerParams(vmem_limit_bytes=ATTEND_LIMIT),
        cost_estimate=pl.CostEstimate(
            flops=4 * fresh * heads * total_keys * HD,
            bytes_accessed=6 << 20,
            transcendentals=fresh * heads * total_keys,
        ),
        name="attend",
    )(carry, pool)
    back = lax.all_to_all(out, ("zh", "core"), split_axis=0, concat_axis=0)
    return back.transpose(1, 0, 2).reshape(tokens, width)


def solution(mesh):
    fine = Mesh(mesh.devices.reshape(SIZES), EVERY)
    whole = P(EVERY, None)
    part = P(("y", "x", "zl"), ("zh", "core"))
    return jax.shard_map(
        local,
        mesh=fine,
        in_specs=(whole, whole, whole, part, part),
        out_specs=whole,
        check_vma=False,
    )
```

```python
import math

import jax
import jax.numpy as jnp
import numpy as np
from jax import lax
from jax.experimental import pallas as pl
from jax.experimental.pallas import tpu as pltpu
from jax.sharding import Mesh
from jax.sharding import PartitionSpec as P

HD = 128
EVERY = ("y", "x", "zl", "zh", "core")
SIZES = (4, 4, 8, 2, 2)
SCALE = HD**-0.5 * math.log2(math.e)
NT = (((1,), (1,)), ((), ()))
F32 = jnp.float32
LIMIT = 60 << 20
SPREAD_LIMIT = 48 << 20
ATTEND_LIMIT = 48 << 20
FRESH_COST = 1 << 30
ARRIVE_COST = 60 << 30
BF16 = jnp.bfloat16
ANY = pl.BlockSpec(memory_space=pl.ANY)
VMEM = pl.BlockSpec(memory_space=pltpu.VMEM)


def peers():
    zh, core = lax.axis_index("zh"), lax.axis_index("core")
    return [a * 2 + b for a in (zh, 1 - zh) for b in (core, 1 - core)]


def pack(qa, ka, va, ksa, vsa, *refs):
    parts, pooled_ref = refs[0:4], refs[4]
    q_ref, k_ref, v_ref, ks_ref, vs_ref, sem = refs[5:]
    loads = zip((ksa, vsa, qa, ka, va), (ks_ref, vs_ref, q_ref, k_ref, v_ref))
    loads = [pltpu.make_async_copy(a, b, sem.at[i]) for i, (a, b) in enumerate(loads)]
    for c in loads:
        c.start()
    mine = ks_ref.shape[1]
    for c in loads[:2]:
        c.wait()
    for j in range(pooled_ref.shape[0]):
        pooled_ref[j, :, 0:mine] = ks_ref[...]
        pooled_ref[j, :, mine : 2 * mine] = vs_ref[...]
    places = peers()
    for t, ref in enumerate((q_ref, k_ref, v_ref)):
        loads[2 + t].wait()
        for p, part in enumerate(parts):
            cols = pl.ds(pl.multiple_of(places[p] * mine, HD), mine)
            part[:, t * mine : (t + 1) * mine] = ref[:, cols]


def spread(line_ref, out_ref, sem):
    copies = [pltpu.make_async_copy(line_ref, out_ref.at[j], sem.at[j]) for j in range(out_ref.shape[0])]
    for c in copies:
        c.start()
    for c in copies:
        c.wait()


def follow(first_ref, ref, out_ref):
    pass


def arrive(near_ref, same_ref, near_out, same_out):
    pass


def attend_fresh(p0, p1, p2, p3, out_ref, part_ref, carry_ref, s_ref, sem, sem_o):
    tokens = part_ref.shape[1]
    mine = part_ref.shape[2] // 3
    heads = mine // HD
    loads = [pltpu.make_async_copy(ref, part_ref.at[i], sem.at[i]) for i, ref in enumerate((p0, p1, p2, p3))]
    stores = []
    for i in range(4):
        rows = pl.ds(i * tokens, tokens)
        stores.append(pltpu.make_async_copy(carry_ref.at[rows], out_ref.at[rows], sem_o.at[i]))
    for c in loads:
        c.start()
    lane = lax.broadcasted_iota(jnp.int32, (tokens, HD), 1)
    steps = [(h, i) for i in range(4) for h in range(heads)]
    tops, stats = {}, {}

    def scores(n):
        h, i = steps[n]
        q = part_ref[i, :, h * HD : (h + 1) * HD]
        top = jnp.full((tokens, HD), -jnp.inf, F32)
        keys = part_ref[:, :, mine + h * HD : mine + (h + 1) * HD].reshape(4 * tokens, HD)
        s = lax.dot_general(q, keys, NT, preferred_element_type=F32)
        s_ref[n % 2] = s
        for d in range(0, 4 * tokens, HD):
            top = jnp.maximum(top, s[:, d : d + HD])
        tops[n] = jnp.max(top, axis=1, keepdims=True)
        carry_ref[i * tokens : (i + 1) * tokens, h * HD : (h + 1) * HD] = q.astype(F32)

    def weigh(n):
        h, i = steps[n]
        rows = slice(i * tokens, (i + 1) * tokens)
        top = tops.pop(n)
        w = jnp.exp2(s_ref[n % 2] * SCALE - top * SCALE)
        sums = jnp.zeros((tokens, HD), F32)
        for d in range(0, 4 * tokens, HD):
            sums = sums + w[:, d : d + HD]
        values = part_ref[:, :, 2 * mine + h * HD : 2 * mine + (h + 1) * HD].reshape(4 * tokens, HD)
        acc = jnp.dot(w.astype(BF16), values, preferred_element_type=F32)
        carry_ref[rows, mine + h * HD : mine + (h + 1) * HD] = acc
        stat = jnp.where(lane == 2 * h, top, stats.get(i, 0.0))
        stats[i] = jnp.where(lane == 2 * h + 1, jnp.sum(sums, axis=1, keepdims=True), stat)
        if h == heads - 1:
            carry_ref[rows, 2 * mine :] = stats.pop(i)
            stores[i].start()

    for c in loads:
        c.wait()
    scores(0)
    for n in range(len(steps)):
        if n + 1 < len(steps):
            scores(n + 1)
        weigh(n)
    for c in stores:
        c.wait()


def attend(carry_ref, pool_ref, out_ref, s_ref):
    tokens, mine = out_ref.shape[1:]
    heads = mine // HD
    blocks, block = pool_ref.shape[0], pool_ref.shape[1]
    stale = blocks * block
    here = lax.axis_index("y") * 4 + lax.axis_index("x")
    first = here * block + lax.axis_index("zl") * (block // 8)
    col = lax.broadcasted_iota(jnp.int32, (tokens, block), 1)
    places = peers()
    steps = [(h, i) for i in range(4) for h in range(heads)]
    tops = {}

    def own(b):
        return (col >= first - b * block) & (col < first - b * block + block // 8)

    def scores(n):
        h, i = steps[n]
        rows = slice(i * tokens, (i + 1) * tokens)
        cs = slice(h * HD, (h + 1) * HD)
        q = carry_ref[rows, cs].astype(BF16)
        before = carry_ref[rows, 2 * mine + 2 * h : 2 * mine + 2 * h + 1]
        top = jnp.broadcast_to(before, (tokens, HD))
        for b in range(0, blocks, 4):
            keys = pool_ref[b : b + 4, :, cs].reshape(4 * block, HD)
            s = lax.dot_general(q, keys, NT, preferred_element_type=F32)
            for d in range(4):
                piece = jnp.where(own(b + d), -jnp.inf, s[:, d * block : (d + 1) * block])
                s_ref[n % 2, :, (b + d) * block : (b + d + 1) * block] = piece
                top = jnp.maximum(top, piece)
        tops[n] = (before, jnp.max(top, axis=1, keepdims=True))

    def weigh(n):
        h, i = steps[n]
        rows = slice(i * tokens, (i + 1) * tokens)
        cs = slice(mine + h * HD, mine + (h + 1) * HD)
        before, top = tops.pop(n)
        shrink = jnp.exp2((before - top) * SCALE)
        top = top * SCALE
        sums = jnp.zeros((tokens, HD), F32)
        acc = carry_ref[rows, cs] * shrink
        for b in range(0, blocks, 4):
            w = jnp.exp2(s_ref[n % 2, :, b * block : (b + 4) * block] * SCALE - top)
            for d in range(4):
                sums = sums + w[:, d * block : (d + 1) * block]
            values = pool_ref[b : b + 4, :, cs].reshape(4 * block, HD)
            acc = acc + jnp.dot(w.astype(BF16), values, preferred_element_type=F32)
        total = carry_ref[rows, 2 * mine + 2 * h + 1 : 2 * mine + 2 * h + 2] * shrink
        total = total + jnp.sum(sums, axis=1, keepdims=True)
        out_ref[places[i], :, h * HD : (h + 1) * HD] = (acc / total).astype(BF16)

    scores(0)
    for n in range(len(steps)):
        if n + 1 < len(steps):
            scores(n + 1)
        weigh(n)


def flips(zh, core):
    pairs = []
    for i in range(math.prod(SIZES)):
        place = list(np.unravel_index(i, SIZES))
        place[3] ^= zh
        place[4] ^= core
        pairs.append((i, int(np.ravel_multi_index(place, SIZES))))
    return pairs


def local(q_fresh, k_fresh, v_fresh, k_stale, v_stale):
    tokens, width = q_fresh.shape
    pooled, mine = k_stale.shape
    heads = mine // HD
    dma = pltpu.SemaphoreType.DMA
    part = jax.ShapeDtypeStruct((tokens, 3 * mine), BF16)
    own, near, same, other, copies = pl.pallas_call(
        pack,
        out_shape=(part,) * 4 + (jax.ShapeDtypeStruct((8, pooled, 2 * mine), BF16),),
        in_specs=[ANY] * 5,
        out_specs=(pl.BlockSpec(),) * 5,
        scratch_shapes=[pltpu.VMEM((tokens, width), BF16)] * 3 + [pltpu.VMEM((pooled, mine), BF16)] * 2 + [dma((5,))],
        compiler_params=pltpu.CompilerParams(vmem_limit_bytes=LIMIT),
        cost_estimate=pl.CostEstimate(flops=0, bytes_accessed=3 << 20, transcendentals=0),
        name="pack",
    )(q_fresh, k_fresh, v_fresh, k_stale, v_stale)
    near = lax.ppermute(near, EVERY, flips(0, 1))
    same = lax.ppermute(same, EVERY, flips(1, 0))
    line = lax.all_to_all(copies, "zl", split_axis=0, concat_axis=0).reshape(8 * pooled, 2 * mine)
    planes = pl.pallas_call(
        spread,
        out_shape=jax.ShapeDtypeStruct((16, 8 * pooled, 2 * mine), BF16),
        in_specs=[VMEM],
        out_specs=ANY,
        scratch_shapes=[dma((16,))],
        compiler_params=pltpu.CompilerParams(vmem_limit_bytes=SPREAD_LIMIT),
        cost_estimate=pl.CostEstimate(flops=0, bytes_accessed=3 << 20, transcendentals=0),
        name="spread",
    )(line)
    other = pl.pallas_call(
        follow,
        out_shape=part,
        in_specs=[ANY, ANY],
        out_specs=ANY,
        input_output_aliases={1: 0},
        compiler_params=pltpu.CompilerParams(vmem_limit_bytes=LIMIT),
        cost_estimate=pl.CostEstimate(flops=0, bytes_accessed=0, transcendentals=0),
        name="follow",
    )(planes, other)
    other = lax.ppermute(other, EVERY, flips(1, 1))
    near, same = pl.pallas_call(
        arrive,
        out_shape=(part, part),
        in_specs=[ANY, ANY],
        out_specs=(ANY, ANY),
        input_output_aliases={0: 0, 1: 1},
        compiler_params=pltpu.CompilerParams(vmem_limit_bytes=LIMIT),
        cost_estimate=pl.CostEstimate(flops=ARRIVE_COST, bytes_accessed=0, transcendentals=0),
        name="arrive",
    )(near, same)
    pool = lax.all_to_all(planes, ("y", "x"), split_axis=0, concat_axis=0)

    fresh = 4 * tokens
    carry = jax.ShapeDtypeStruct((fresh, 2 * mine + HD), F32)
    carry = pl.pallas_call(
        attend_fresh,
        out_shape=carry,
        in_specs=[ANY] * 4,
        out_specs=ANY,
        scratch_shapes=[
            pltpu.VMEM((4, tokens, 3 * mine), BF16),
            pltpu.VMEM(carry.shape, F32),
            pltpu.VMEM((2, tokens, fresh), F32),
            dma((4,)),
            dma((4,)),
        ],
        compiler_params=pltpu.CompilerParams(vmem_limit_bytes=LIMIT),
        cost_estimate=pl.CostEstimate(flops=FRESH_COST, bytes_accessed=3 << 20, transcendentals=0),
        name="attend_fresh",
    )(own, near, same, other)
    total_keys = 16 * 8 * pooled
    out = pl.pallas_call(
        attend,
        out_shape=jax.ShapeDtypeStruct((4, tokens, mine), BF16),
        in_specs=[VMEM, VMEM],
        out_specs=VMEM,
        scratch_shapes=[pltpu.VMEM((2, tokens, total_keys), F32)],
        compiler_params=pltpu.CompilerParams(vmem_limit_bytes=ATTEND_LIMIT),
        cost_estimate=pl.CostEstimate(
            flops=4 * fresh * heads * total_keys * HD,
            bytes_accessed=6 << 20,
            transcendentals=fresh * heads * total_keys,
        ),
        name="attend",
    )(carry, pool)
    back = lax.all_to_all(out, ("zh", "core"), split_axis=0, concat_axis=0)
    return back.transpose(1, 0, 2).reshape(tokens, width)


def solution(mesh):
    fine = Mesh(mesh.devices.reshape(SIZES), EVERY)
    whole = P(EVERY, None)
    part = P(("y", "x", "zl"), ("zh", "core"))
    return jax.shard_map(
        local,
        mesh=fine,
        in_specs=(whole, whole, whole, part, part),
        out_specs=whole,
        check_vma=False,
    )
```

```python
import math

import jax
import jax.numpy as jnp
import numpy as np
from jax import lax
from jax.experimental import pallas as pl
from jax.experimental.pallas import tpu as pltpu
from jax.sharding import Mesh
from jax.sharding import PartitionSpec as P

HD = 128
EVERY = ("y", "x", "zl", "zh", "core")
SIZES = (4, 4, 8, 2, 2)
SCALE = HD**-0.5 * math.log2(math.e)
NT = (((1,), (1,)), ((), ()))
F32 = jnp.float32
LIMIT = 60 << 20
SPREAD_LIMIT = 48 << 20
ATTEND_LIMIT = 48 << 20
EARLY_COST = 60 << 30
BF16 = jnp.bfloat16
ANY = pl.BlockSpec(memory_space=pl.ANY)
VMEM = pl.BlockSpec(memory_space=pltpu.VMEM)


def peers():
    zh, core = lax.axis_index("zh"), lax.axis_index("core")
    return [a * 2 + b for a in (zh, 1 - zh) for b in (core, 1 - core)]


def pack(qa, ka, va, ksa, vsa, *refs):
    parts, pooled_ref = refs[0:4], refs[4]
    q_ref, k_ref, v_ref, ks_ref, vs_ref, sem = refs[5:]
    loads = zip((ksa, vsa, qa, ka, va), (ks_ref, vs_ref, q_ref, k_ref, v_ref))
    loads = [pltpu.make_async_copy(a, b, sem.at[i]) for i, (a, b) in enumerate(loads)]
    for c in loads:
        c.start()
    mine = ks_ref.shape[1]
    for c in loads[:2]:
        c.wait()
    for j in range(pooled_ref.shape[0]):
        pooled_ref[j, :, 0:mine] = ks_ref[...]
        pooled_ref[j, :, mine : 2 * mine] = vs_ref[...]
    places = peers()
    for t, ref in enumerate((q_ref, k_ref, v_ref)):
        loads[2 + t].wait()
        for p, part in enumerate(parts):
            cols = pl.ds(pl.multiple_of(places[p] * mine, HD), mine)
            part[:, t * mine : (t + 1) * mine] = ref[:, cols]


def spread(line_ref, out_ref, sem):
    copies = [pltpu.make_async_copy(line_ref, out_ref.at[j], sem.at[j]) for j in range(out_ref.shape[0])]
    for c in copies:
        c.start()
    for c in copies:
        c.wait()


def follow(first_ref, ref, out_ref):
    pass


def attend_early(p0, p1, p2, out_ref, kv_ref, part_ref, carry_ref, s_ref, sem, sem_o):
    parts, tokens = part_ref.shape[:2]
    mine = part_ref.shape[2] // 3
    heads = mine // HD
    loads = [pltpu.make_async_copy(ref, part_ref.at[i], sem.at[i]) for i, ref in enumerate((p0, p1, p2))]
    stores = []
    for i in range(parts):
        rows = pl.ds(i * tokens, tokens)
        stores.append(pltpu.make_async_copy(carry_ref.at[rows], out_ref.at[rows], sem_o.at[i]))
    for i in range(parts):
        rows = pl.ds(i * tokens, tokens)
        stores.append(pltpu.make_async_copy(part_ref.at[i, :, mine:], kv_ref.at[rows], sem_o.at[parts + i]))
    for c in loads:
        c.start()
    lane = lax.broadcasted_iota(jnp.int32, (tokens, HD), 1)
    steps = [(h, i) for i in range(parts) for h in range(heads)]
    tops, stats = {}, {}

    def scores(n):
        h, i = steps[n]
        q = part_ref[i, :, h * HD : (h + 1) * HD]
        top = jnp.full((tokens, HD), -jnp.inf, F32)
        keys = part_ref[:, :, mine + h * HD : mine + (h + 1) * HD].reshape(parts * tokens, HD)
        s = lax.dot_general(q, keys, NT, preferred_element_type=F32)
        s_ref[n % 2] = s
        for d in range(0, parts * tokens, HD):
            top = jnp.maximum(top, s[:, d : d + HD])
        tops[n] = jnp.max(top, axis=1, keepdims=True)
        carry_ref[i * tokens : (i + 1) * tokens, h * HD : (h + 1) * HD] = q.astype(F32)

    def weigh(n):
        h, i = steps[n]
        rows = slice(i * tokens, (i + 1) * tokens)
        top = tops.pop(n)
        w = jnp.exp2(s_ref[n % 2] * SCALE - top * SCALE)
        sums = jnp.zeros((tokens, HD), F32)
        for d in range(0, parts * tokens, HD):
            sums = sums + w[:, d : d + HD]
        values = part_ref[:, :, 2 * mine + h * HD : 2 * mine + (h + 1) * HD].reshape(parts * tokens, HD)
        acc = jnp.dot(w.astype(BF16), values, preferred_element_type=F32)
        carry_ref[rows, mine + h * HD : mine + (h + 1) * HD] = acc
        stat = jnp.where(lane == 2 * h, top, stats.get(i, 0.0))
        stats[i] = jnp.where(lane == 2 * h + 1, jnp.sum(sums, axis=1, keepdims=True), stat)
        if h == heads - 1:
            carry_ref[rows, 2 * mine :] = stats.pop(i)
            stores[i].start()

    for c in loads:
        c.wait()
    for c in stores[parts:]:
        c.start()
    scores(0)
    for n in range(len(steps)):
        if n + 1 < len(steps):
            scores(n + 1)
        weigh(n)
    for c in stores:
        c.wait()


def attend(carry_ref, kv_ref, last_ref, pool_ref, out_ref, s_ref):
    tokens, mine = out_ref.shape[1:]
    heads = mine // HD
    blocks, block = pool_ref.shape[0], pool_ref.shape[1]
    stale = blocks * block
    here = lax.axis_index("y") * 4 + lax.axis_index("x")
    first = here * block + lax.axis_index("zl") * (block // 8)
    col = lax.broadcasted_iota(jnp.int32, (tokens, block), 1)
    places = peers()
    steps = [(h, i) for i in range(4) for h in range(heads)]
    tops = {}

    def own(b):
        return (col >= first - b * block) & (col < first - b * block + block // 8)

    def extra(h, i, t):
        late = [last_ref[:, (1 + t) * mine + h * HD : (1 + t) * mine + (h + 1) * HD]]
        early = [kv_ref[:, t * mine + h * HD : t * mine + (h + 1) * HD]]
        return early + late if i == 3 else late

    def scores(n):
        h, i = steps[n]
        cs = slice(h * HD, (h + 1) * HD)
        if i == 3:
            q = last_ref[:, cs]
        else:
            q = carry_ref[i * tokens : (i + 1) * tokens, cs].astype(BF16)
        top = jnp.full((tokens, HD), -jnp.inf, F32)
        for b in range(0, blocks, 4):
            keys = pool_ref[b : b + 4, :, cs].reshape(4 * block, HD)
            s = lax.dot_general(q, keys, NT, preferred_element_type=F32)
            for d in range(4):
                piece = jnp.where(own(b + d), -jnp.inf, s[:, d * block : (d + 1) * block])
                s_ref[n % 2, :, (b + d) * block : (b + d + 1) * block] = piece
                top = jnp.maximum(top, piece)
        at = stale
        for keys in extra(h, i, 0):
            s = lax.dot_general(q, keys, NT, preferred_element_type=F32)
            s_ref[n % 2, :, at : at + keys.shape[0]] = s
            at += keys.shape[0]
            for d in range(0, keys.shape[0], HD):
                top = jnp.maximum(top, s[:, d : d + HD])
        tops[n] = jnp.max(top, axis=1, keepdims=True)

    def weigh(n):
        h, i = steps[n]
        rows = slice(i * tokens, (i + 1) * tokens)
        cs = slice(mine + h * HD, mine + (h + 1) * HD)
        top = tops.pop(n)
        if i == 3:
            acc = jnp.zeros((tokens, HD), F32)
            total = jnp.zeros((tokens, 1), F32)
        else:
            before = carry_ref[rows, 2 * mine + 2 * h : 2 * mine + 2 * h + 1]
            top = jnp.maximum(top, before)
            shrink = jnp.exp2((before - top) * SCALE)
            acc = carry_ref[rows, cs] * shrink
            total = carry_ref[rows, 2 * mine + 2 * h + 1 : 2 * mine + 2 * h + 2] * shrink
        top = top * SCALE
        sums = jnp.zeros((tokens, HD), F32)
        values = [pool_ref[b : b + 4, :, cs].reshape(4 * block, HD) for b in range(0, blocks, 4)]
        at = 0
        for v in values + extra(h, i, 1):
            width = v.shape[0]
            w = jnp.exp2(s_ref[n % 2, :, at : at + width] * SCALE - top)
            at += width
            for d in range(0, width, HD):
                sums = sums + w[:, d : d + HD]
            acc = acc + jnp.dot(w.astype(BF16), v, preferred_element_type=F32)
        total = total + jnp.sum(sums, axis=1, keepdims=True)
        out_ref[places[i], :, h * HD : (h + 1) * HD] = (acc / total).astype(BF16)

    scores(0)
    for n in range(len(steps)):
        if n + 1 < len(steps):
            scores(n + 1)
        weigh(n)


def flips(zh, core):
    pairs = []
    for i in range(math.prod(SIZES)):
        place = list(np.unravel_index(i, SIZES))
        place[3] ^= zh
        place[4] ^= core
        pairs.append((i, int(np.ravel_multi_index(place, SIZES))))
    return pairs


def local(q_fresh, k_fresh, v_fresh, k_stale, v_stale):
    tokens, width = q_fresh.shape
    pooled, mine = k_stale.shape
    heads = mine // HD
    dma = pltpu.SemaphoreType.DMA
    part = jax.ShapeDtypeStruct((tokens, 3 * mine), BF16)
    own, near, same, other, copies = pl.pallas_call(
        pack,
        out_shape=(part,) * 4 + (jax.ShapeDtypeStruct((8, pooled, 2 * mine), BF16),),
        in_specs=[ANY] * 5,
        out_specs=(pl.BlockSpec(),) * 5,
        scratch_shapes=[pltpu.VMEM((tokens, width), BF16)] * 3 + [pltpu.VMEM((pooled, mine), BF16)] * 2 + [dma((5,))],
        compiler_params=pltpu.CompilerParams(vmem_limit_bytes=LIMIT),
        cost_estimate=pl.CostEstimate(flops=0, bytes_accessed=3 << 20, transcendentals=0),
        name="pack",
    )(q_fresh, k_fresh, v_fresh, k_stale, v_stale)
    near = lax.ppermute(near, EVERY, flips(0, 1))
    same = lax.ppermute(same, EVERY, flips(1, 0))
    line = lax.all_to_all(copies, "zl", split_axis=0, concat_axis=0).reshape(8 * pooled, 2 * mine)
    planes = pl.pallas_call(
        spread,
        out_shape=jax.ShapeDtypeStruct((16, 8 * pooled, 2 * mine), BF16),
        in_specs=[VMEM],
        out_specs=ANY,
        scratch_shapes=[dma((16,))],
        compiler_params=pltpu.CompilerParams(vmem_limit_bytes=SPREAD_LIMIT),
        cost_estimate=pl.CostEstimate(flops=0, bytes_accessed=3 << 20, transcendentals=0),
        name="spread",
    )(line)
    other = pl.pallas_call(
        follow,
        out_shape=part,
        in_specs=[ANY, ANY],
        out_specs=ANY,
        input_output_aliases={1: 0},
        compiler_params=pltpu.CompilerParams(vmem_limit_bytes=LIMIT),
        cost_estimate=pl.CostEstimate(flops=0, bytes_accessed=0, transcendentals=0),
        name="follow",
    )(planes, other)
    other = lax.ppermute(other, EVERY, flips(1, 1))
    pool = lax.all_to_all(planes, ("y", "x"), split_axis=0, concat_axis=0)

    early = 3 * tokens
    carry = jax.ShapeDtypeStruct((early, 2 * mine + HD), F32)
    carry, kv = pl.pallas_call(
        attend_early,
        out_shape=(carry, jax.ShapeDtypeStruct((early, 2 * mine), BF16)),
        in_specs=[ANY] * 3,
        out_specs=(ANY, ANY),
        scratch_shapes=[
            pltpu.VMEM((3, tokens, 3 * mine), BF16),
            pltpu.VMEM(carry.shape, F32),
            pltpu.VMEM((2, tokens, early), F32),
            dma((3,)),
            dma((6,)),
        ],
        compiler_params=pltpu.CompilerParams(vmem_limit_bytes=LIMIT),
        cost_estimate=pl.CostEstimate(flops=EARLY_COST, bytes_accessed=3 << 20, transcendentals=0),
        name="attend_early",
    )(own, near, same)
    fresh = 4 * tokens
    total_keys = 16 * 8 * pooled + fresh
    out = pl.pallas_call(
        attend,
        out_shape=jax.ShapeDtypeStruct((4, tokens, mine), BF16),
        in_specs=[VMEM] * 4,
        out_specs=VMEM,
        scratch_shapes=[pltpu.VMEM((2, tokens, total_keys), F32)],
        compiler_params=pltpu.CompilerParams(vmem_limit_bytes=ATTEND_LIMIT),
        cost_estimate=pl.CostEstimate(
            flops=4 * fresh * heads * total_keys * HD,
            bytes_accessed=6 << 20,
            transcendentals=fresh * heads * total_keys,
        ),
        name="attend",
    )(carry, kv, other, pool)
    back = lax.all_to_all(out, ("zh", "core"), split_axis=0, concat_axis=0)
    return back.transpose(1, 0, 2).reshape(tokens, width)


def solution(mesh):
    fine = Mesh(mesh.devices.reshape(SIZES), EVERY)
    whole = P(EVERY, None)
    part = P(("y", "x", "zl"), ("zh", "core"))
    return jax.shard_map(
        local,
        mesh=fine,
        in_specs=(whole, whole, whole, part, part),
        out_specs=whole,
        check_vma=False,
    )
```

```python
import functools
import math

import jax
import jax.numpy as jnp
import numpy as np
from jax import lax
from jax.experimental import pallas as pl
from jax.experimental.pallas import tpu as pltpu
from jax.sharding import Mesh
from jax.sharding import PartitionSpec as P

HD = 128
EVERY = ("y", "x", "zl", "zh", "core")
SIZES = (4, 4, 8, 2, 2)
SCALE = HD**-0.5 * math.log2(math.e)
NT = (((1,), (1,)), ((), ()))
F32 = jnp.float32
LIMIT = 60 << 20
SPREAD_LIMIT = 48 << 20
ATTEND_LIMIT = 48 << 20
EARLY_COST = 60 << 30
BF16 = jnp.bfloat16
ANY = pl.BlockSpec(memory_space=pl.ANY)
VMEM = pl.BlockSpec(memory_space=pltpu.VMEM)


def peers():
    zh, core = lax.axis_index("zh"), lax.axis_index("core")
    return [a * 2 + b for a in (zh, 1 - zh) for b in (core, 1 - core)]


def pack(qa, ka, va, ksa, vsa, *refs):
    parts, pooled_ref = refs[0:4], refs[4]
    q_ref, k_ref, v_ref, ks_ref, vs_ref, sem = refs[5:]
    loads = zip((ksa, vsa, qa, ka, va), (ks_ref, vs_ref, q_ref, k_ref, v_ref))
    loads = [pltpu.make_async_copy(a, b, sem.at[i]) for i, (a, b) in enumerate(loads)]
    for c in loads:
        c.start()
    mine = ks_ref.shape[1]
    for c in loads[:2]:
        c.wait()
    for j in range(pooled_ref.shape[0]):
        pooled_ref[j, :, 0:mine] = ks_ref[...]
        pooled_ref[j, :, mine : 2 * mine] = vs_ref[...]
    places = peers()
    for t, ref in enumerate((q_ref, k_ref, v_ref)):
        loads[2 + t].wait()
        for p, part in enumerate(parts):
            cols = pl.ds(pl.multiple_of(places[p] * mine, HD), mine)
            part[:, t * mine : (t + 1) * mine] = ref[:, cols]


def spread(line_ref, out_ref, sem):
    copies = [pltpu.make_async_copy(line_ref, out_ref.at[j], sem.at[j]) for j in range(out_ref.shape[0])]
    for c in copies:
        c.start()
    for c in copies:
        c.wait()


def follow(first_ref, ref, out_ref):
    pass


def attend_early(p0, p1, p2, out_ref, kv_ref, part_ref, carry_ref, s_ref, sem, sem_o):
    parts, tokens = part_ref.shape[:2]
    mine = part_ref.shape[2] // 3
    heads = mine // HD
    loads = [pltpu.make_async_copy(ref, part_ref.at[i], sem.at[i]) for i, ref in enumerate((p0, p1, p2))]
    stores = []
    for i in range(parts):
        rows = pl.ds(i * tokens, tokens)
        stores.append(pltpu.make_async_copy(carry_ref.at[rows], out_ref.at[rows], sem_o.at[i]))
    for i in range(parts):
        rows = pl.ds(i * tokens, tokens)
        stores.append(pltpu.make_async_copy(part_ref.at[i, :, mine:], kv_ref.at[rows], sem_o.at[parts + i]))
    for c in loads:
        c.start()
    lane = lax.broadcasted_iota(jnp.int32, (tokens, HD), 1)
    steps = [(h, i) for i in range(parts) for h in range(heads)]
    tops, stats = {}, {}

    def scores(n):
        h, i = steps[n]
        q = part_ref[i, :, h * HD : (h + 1) * HD]
        top = jnp.full((tokens, HD), -jnp.inf, F32)
        keys = part_ref[:, :, mine + h * HD : mine + (h + 1) * HD].reshape(parts * tokens, HD)
        s = lax.dot_general(q, keys, NT, preferred_element_type=F32)
        s_ref[n % 2] = s
        for d in range(0, parts * tokens, HD):
            top = jnp.maximum(top, s[:, d : d + HD])
        tops[n] = jnp.max(top, axis=1, keepdims=True)
        carry_ref[i * tokens : (i + 1) * tokens, h * HD : (h + 1) * HD] = q.astype(F32)

    def weigh(n):
        h, i = steps[n]
        rows = slice(i * tokens, (i + 1) * tokens)
        top = tops.pop(n)
        w = jnp.exp2(s_ref[n % 2] * SCALE - top * SCALE)
        sums = jnp.zeros((tokens, HD), F32)
        for d in range(0, parts * tokens, HD):
            sums = sums + w[:, d : d + HD]
        values = part_ref[:, :, 2 * mine + h * HD : 2 * mine + (h + 1) * HD].reshape(parts * tokens, HD)
        acc = jnp.dot(w.astype(BF16), values, preferred_element_type=F32)
        carry_ref[rows, mine + h * HD : mine + (h + 1) * HD] = acc
        stat = jnp.where(lane == 2 * h, top, stats.get(i, 0.0))
        stats[i] = jnp.where(lane == 2 * h + 1, jnp.sum(sums, axis=1, keepdims=True), stat)
        if h == heads - 1:
            carry_ref[rows, 2 * mine :] = stats.pop(i)
            stores[i].start()

    for c in loads:
        c.wait()
    for c in stores[parts:]:
        c.start()
    scores(0)
    for n in range(len(steps)):
        if n + 1 < len(steps):
            scores(n + 1)
        weigh(n)
    for c in stores:
        c.wait()


def attend(parts, carry_ref, kv_ref, last_ref, pool_ref, *refs):
    outs, s_ref = refs[:-1], refs[-1]
    tokens, mine = outs[0].shape
    heads = mine // HD
    blocks, block = pool_ref.shape[0], pool_ref.shape[1]
    stale = blocks * block
    here = lax.axis_index("y") * 4 + lax.axis_index("x")
    first = here * block + lax.axis_index("zl") * (block // 8)
    col = lax.broadcasted_iota(jnp.int32, (tokens, block), 1)
    steps = [(h, i) for i in parts for h in range(heads)]
    tops = {}

    def own(b):
        return (col >= first - b * block) & (col < first - b * block + block // 8)

    def extra(h, i, t):
        late = [last_ref[:, (1 + t) * mine + h * HD : (1 + t) * mine + (h + 1) * HD]]
        early = [kv_ref[:, t * mine + h * HD : t * mine + (h + 1) * HD]]
        return early + late if i == 3 else late

    def scores(n):
        h, i = steps[n]
        cs = slice(h * HD, (h + 1) * HD)
        if i == 3:
            q = last_ref[:, cs]
        else:
            q = carry_ref[i * tokens : (i + 1) * tokens, cs].astype(BF16)
        top = jnp.full((tokens, HD), -jnp.inf, F32)
        for b in range(0, blocks, 4):
            keys = pool_ref[b : b + 4, :, cs].reshape(4 * block, HD)
            s = lax.dot_general(q, keys, NT, preferred_element_type=F32)
            for d in range(4):
                piece = jnp.where(own(b + d), -jnp.inf, s[:, d * block : (d + 1) * block])
                s_ref[n % 2, :, (b + d) * block : (b + d + 1) * block] = piece
                top = jnp.maximum(top, piece)
        at = stale
        for keys in extra(h, i, 0):
            s = lax.dot_general(q, keys, NT, preferred_element_type=F32)
            s_ref[n % 2, :, at : at + keys.shape[0]] = s
            at += keys.shape[0]
            for d in range(0, keys.shape[0], HD):
                top = jnp.maximum(top, s[:, d : d + HD])
        tops[n] = jnp.max(top, axis=1, keepdims=True)

    def weigh(n):
        h, i = steps[n]
        rows = slice(i * tokens, (i + 1) * tokens)
        cs = slice(mine + h * HD, mine + (h + 1) * HD)
        top = tops.pop(n)
        if i == 3:
            acc = jnp.zeros((tokens, HD), F32)
            total = jnp.zeros((tokens, 1), F32)
        else:
            before = carry_ref[rows, 2 * mine + 2 * h : 2 * mine + 2 * h + 1]
            top = jnp.maximum(top, before)
            shrink = jnp.exp2((before - top) * SCALE)
            acc = carry_ref[rows, cs] * shrink
            total = carry_ref[rows, 2 * mine + 2 * h + 1 : 2 * mine + 2 * h + 2] * shrink
        top = top * SCALE
        sums = jnp.zeros((tokens, HD), F32)
        values = [pool_ref[b : b + 4, :, cs].reshape(4 * block, HD) for b in range(0, blocks, 4)]
        at = 0
        for v in values + extra(h, i, 1):
            width = v.shape[0]
            w = jnp.exp2(s_ref[n % 2, :, at : at + width] * SCALE - top)
            at += width
            for d in range(0, width, HD):
                sums = sums + w[:, d : d + HD]
            acc = acc + jnp.dot(w.astype(BF16), v, preferred_element_type=F32)
        total = total + jnp.sum(sums, axis=1, keepdims=True)
        outs[parts.index(i)][:, h * HD : (h + 1) * HD] = (acc / total).astype(BF16)

    scores(0)
    for n in range(len(steps)):
        if n + 1 < len(steps):
            scores(n + 1)
        weigh(n)


def unpack(p0, p1, p2, p3, out_ref):
    mine = p0.shape[1]
    for place, ref in zip(peers(), (p0, p1, p2, p3)):
        out_ref[:, pl.ds(pl.multiple_of(place * mine, HD), mine)] = ref[...]


def flips(zh, core):
    pairs = []
    for i in range(math.prod(SIZES)):
        place = list(np.unravel_index(i, SIZES))
        place[3] ^= zh
        place[4] ^= core
        pairs.append((i, int(np.ravel_multi_index(place, SIZES))))
    return pairs


def local(q_fresh, k_fresh, v_fresh, k_stale, v_stale):
    tokens, width = q_fresh.shape
    pooled, mine = k_stale.shape
    heads = mine // HD
    dma = pltpu.SemaphoreType.DMA
    part = jax.ShapeDtypeStruct((tokens, 3 * mine), BF16)
    own, near, same, other, copies = pl.pallas_call(
        pack,
        out_shape=(part,) * 4 + (jax.ShapeDtypeStruct((8, pooled, 2 * mine), BF16),),
        in_specs=[ANY] * 5,
        out_specs=(pl.BlockSpec(),) * 5,
        scratch_shapes=[pltpu.VMEM((tokens, width), BF16)] * 3 + [pltpu.VMEM((pooled, mine), BF16)] * 2 + [dma((5,))],
        compiler_params=pltpu.CompilerParams(vmem_limit_bytes=LIMIT),
        cost_estimate=pl.CostEstimate(flops=0, bytes_accessed=3 << 20, transcendentals=0),
        name="pack",
    )(q_fresh, k_fresh, v_fresh, k_stale, v_stale)
    near = lax.ppermute(near, EVERY, flips(0, 1))
    same = lax.ppermute(same, EVERY, flips(1, 0))
    line = lax.all_to_all(copies, "zl", split_axis=0, concat_axis=0).reshape(8 * pooled, 2 * mine)
    planes = pl.pallas_call(
        spread,
        out_shape=jax.ShapeDtypeStruct((16, 8 * pooled, 2 * mine), BF16),
        in_specs=[VMEM],
        out_specs=ANY,
        scratch_shapes=[dma((16,))],
        compiler_params=pltpu.CompilerParams(vmem_limit_bytes=SPREAD_LIMIT),
        cost_estimate=pl.CostEstimate(flops=0, bytes_accessed=3 << 20, transcendentals=0),
        name="spread",
    )(line)
    other = pl.pallas_call(
        follow,
        out_shape=part,
        in_specs=[ANY, ANY],
        out_specs=ANY,
        input_output_aliases={1: 0},
        compiler_params=pltpu.CompilerParams(vmem_limit_bytes=LIMIT),
        cost_estimate=pl.CostEstimate(flops=0, bytes_accessed=0, transcendentals=0),
        name="follow",
    )(planes, other)
    other = lax.ppermute(other, EVERY, flips(1, 1))
    pool = lax.all_to_all(planes, ("y", "x"), split_axis=0, concat_axis=0)

    early = 3 * tokens
    carry = jax.ShapeDtypeStruct((early, 2 * mine + HD), F32)
    carry, kv = pl.pallas_call(
        attend_early,
        out_shape=(carry, jax.ShapeDtypeStruct((early, 2 * mine), BF16)),
        in_specs=[ANY] * 3,
        out_specs=(ANY, ANY),
        scratch_shapes=[
            pltpu.VMEM((3, tokens, 3 * mine), BF16),
            pltpu.VMEM(carry.shape, F32),
            pltpu.VMEM((2, tokens, early), F32),
            dma((3,)),
            dma((6,)),
        ],
        compiler_params=pltpu.CompilerParams(vmem_limit_bytes=LIMIT),
        cost_estimate=pl.CostEstimate(flops=EARLY_COST, bytes_accessed=3 << 20, transcendentals=0),
        name="attend_early",
    )(own, near, same)
    fresh = 4 * tokens
    total_keys = 16 * 8 * pooled + fresh
    block = jax.ShapeDtypeStruct((tokens, mine), BF16)

    def finish(parts):
        return pl.pallas_call(
            functools.partial(attend, parts),
            out_shape=(block, block),
            in_specs=[VMEM] * 4,
            out_specs=(VMEM, VMEM),
            scratch_shapes=[pltpu.VMEM((2, tokens, total_keys), F32)],
            compiler_params=pltpu.CompilerParams(vmem_limit_bytes=ATTEND_LIMIT),
            cost_estimate=pl.CostEstimate(
                flops=2 * fresh * heads * total_keys * HD,
                bytes_accessed=6 << 20,
                transcendentals=fresh * heads * total_keys // 2,
            ),
            name="attend",
        )(carry, kv, other, pool)

    same, far = finish((2, 3))
    same = lax.ppermute(same, EVERY, flips(1, 0))
    far = lax.ppermute(far, EVERY, flips(1, 1))
    own, near = finish((0, 1))
    near = lax.ppermute(near, EVERY, flips(0, 1))
    return pl.pallas_call(
        unpack,
        out_shape=jax.ShapeDtypeStruct((tokens, width), BF16),
        in_specs=[VMEM] * 4,
        out_specs=VMEM,
        compiler_params=pltpu.CompilerParams(vmem_limit_bytes=SPREAD_LIMIT),
        cost_estimate=pl.CostEstimate(flops=0, bytes_accessed=1 << 20, transcendentals=0),
        name="unpack",
    )(own, near, same, far)


def solution(mesh):
    fine = Mesh(mesh.devices.reshape(SIZES), EVERY)
    whole = P(EVERY, None)
    part = P(("y", "x", "zl"), ("zh", "core"))
    return jax.shard_map(
        local,
        mesh=fine,
        in_specs=(whole, whole, whole, part, part),
        out_specs=whole,
        check_vma=False,
    )
```

```python
import functools
import math

import jax
import jax.numpy as jnp
import numpy as np
from jax import lax
from jax.experimental import pallas as pl
from jax.experimental.pallas import tpu as pltpu
from jax.sharding import Mesh
from jax.sharding import PartitionSpec as P

HD = 128
EVERY = ("y", "x", "zl", "zh", "core")
SIZES = (4, 4, 8, 2, 2)
SCALE = HD**-0.5 * math.log2(math.e)
NT = (((1,), (1,)), ((), ()))
F32 = jnp.float32
LIMIT = 60 << 20
SPREAD_LIMIT = 48 << 20
ATTEND_LIMIT = 48 << 20
EARLY_COST = 60 << 30
BF16 = jnp.bfloat16
ANY = pl.BlockSpec(memory_space=pl.ANY)
VMEM = pl.BlockSpec(memory_space=pltpu.VMEM)


def peers():
    zh, core = lax.axis_index("zh"), lax.axis_index("core")
    return [a * 2 + b for a in (zh, 1 - zh) for b in (core, 1 - core)]


def pack(qa, ka, va, ksa, vsa, *refs):
    parts, pooled_ref = refs[0:4], refs[4]
    q_ref, k_ref, v_ref, ks_ref, vs_ref, sem = refs[5:]
    loads = zip((ksa, vsa, qa, ka, va), (ks_ref, vs_ref, q_ref, k_ref, v_ref))
    loads = [pltpu.make_async_copy(a, b, sem.at[i]) for i, (a, b) in enumerate(loads)]
    for c in loads:
        c.start()
    mine = ks_ref.shape[1]
    for c in loads[:2]:
        c.wait()
    for j in range(pooled_ref.shape[0]):
        pooled_ref[j, :, 0:mine] = ks_ref[...]
        pooled_ref[j, :, mine : 2 * mine] = vs_ref[...]
    places = peers()
    for t, ref in enumerate((q_ref, k_ref, v_ref)):
        loads[2 + t].wait()
        for p, part in enumerate(parts):
            cols = pl.ds(pl.multiple_of(places[p] * mine, HD), mine)
            part[:, t * mine : (t + 1) * mine] = ref[:, cols]


def landed(same_ref, far_ref, same_out, far_out):
    pass


def spread(line_ref, out_ref, sem):
    copies = [pltpu.make_async_copy(line_ref, out_ref.at[j], sem.at[j]) for j in range(out_ref.shape[0])]
    for c in copies:
        c.start()
    for c in copies:
        c.wait()


def follow(first_ref, ref, out_ref):
    pass


def attend_early(p0, p1, p2, out_ref, far_ref, kv_ref, part_ref, carry_ref, s_ref, sem, sem_o):
    parts, tokens = part_ref.shape[:2]
    mine = part_ref.shape[2] // 3
    heads = mine // HD
    loads = [pltpu.make_async_copy(ref, part_ref.at[i], sem.at[i]) for i, ref in enumerate((p0, p1, p2))]
    stores = []
    for i in range(parts):
        rows = pl.ds(i * tokens, tokens)
        to = far_ref if i == 2 else out_ref.at[rows]
        stores.append(pltpu.make_async_copy(carry_ref.at[rows], to, sem_o.at[i]))
    for i in range(parts):
        rows = pl.ds(i * tokens, tokens)
        stores.append(pltpu.make_async_copy(part_ref.at[i, :, mine:], kv_ref.at[rows], sem_o.at[parts + i]))
    for c in loads:
        c.start()
    lane = lax.broadcasted_iota(jnp.int32, (tokens, HD), 1)
    steps = [(h, i) for i in range(parts) for h in range(heads)]
    tops, stats = {}, {}

    def scores(n):
        h, i = steps[n]
        q = part_ref[i, :, h * HD : (h + 1) * HD]
        top = jnp.full((tokens, HD), -jnp.inf, F32)
        keys = part_ref[:, :, mine + h * HD : mine + (h + 1) * HD].reshape(parts * tokens, HD)
        s = lax.dot_general(q, keys, NT, preferred_element_type=F32)
        s_ref[n % 2] = s
        for d in range(0, parts * tokens, HD):
            top = jnp.maximum(top, s[:, d : d + HD])
        tops[n] = jnp.max(top, axis=1, keepdims=True)
        carry_ref[i * tokens : (i + 1) * tokens, h * HD : (h + 1) * HD] = q.astype(F32)

    def weigh(n):
        h, i = steps[n]
        rows = slice(i * tokens, (i + 1) * tokens)
        top = tops.pop(n)
        w = jnp.exp2(s_ref[n % 2] * SCALE - top * SCALE)
        sums = jnp.zeros((tokens, HD), F32)
        for d in range(0, parts * tokens, HD):
            sums = sums + w[:, d : d + HD]
        values = part_ref[:, :, 2 * mine + h * HD : 2 * mine + (h + 1) * HD].reshape(parts * tokens, HD)
        acc = jnp.dot(w.astype(BF16), values, preferred_element_type=F32)
        carry_ref[rows, mine + h * HD : mine + (h + 1) * HD] = acc
        stat = jnp.where(lane == 2 * h, top, stats.get(i, 0.0))
        stats[i] = jnp.where(lane == 2 * h + 1, jnp.sum(sums, axis=1, keepdims=True), stat)
        if h == heads - 1:
            carry_ref[rows, 2 * mine :] = stats.pop(i)
            stores[i].start()

    for c in loads:
        c.wait()
    for c in stores[parts:]:
        c.start()
    scores(0)
    for n in range(len(steps)):
        if n + 1 < len(steps):
            scores(n + 1)
        weigh(n)
    for c in stores:
        c.wait()


def attend(parts, carry_ref, kv_ref, last_ref, pool_ref, *refs):
    outs, s_ref = refs[:-1], refs[-1]
    tokens, mine = outs[0].shape
    heads = mine // HD
    blocks, block = pool_ref.shape[0], pool_ref.shape[1]
    stale = blocks * block
    here = lax.axis_index("y") * 4 + lax.axis_index("x")
    first = here * block + lax.axis_index("zl") * (block // 8)
    col = lax.broadcasted_iota(jnp.int32, (tokens, block), 1)
    steps = [(h, i) for i in parts for h in range(heads)]
    tops = {}

    def own(b):
        return (col >= first - b * block) & (col < first - b * block + block // 8)

    def place(i):
        return slice((i - parts[0]) * tokens, (i - parts[0] + 1) * tokens)

    def extra(h, i, t):
        late = [last_ref[:, (1 + t) * mine + h * HD : (1 + t) * mine + (h + 1) * HD]]
        if i != 3:
            return late
        return [kv_ref[:, t * mine + h * HD : t * mine + (h + 1) * HD]] + late

    def scores(n):
        h, i = steps[n]
        cs = slice(h * HD, (h + 1) * HD)
        if i == 3:
            q = last_ref[:, cs]
        else:
            q = carry_ref[place(i), cs].astype(BF16)
        top = jnp.full((tokens, HD), -jnp.inf, F32)
        for b in range(0, blocks, 4):
            keys = pool_ref[b : b + 4, :, cs].reshape(4 * block, HD)
            s = lax.dot_general(q, keys, NT, preferred_element_type=F32)
            for d in range(4):
                piece = jnp.where(own(b + d), -jnp.inf, s[:, d * block : (d + 1) * block])
                s_ref[n % 2, :, (b + d) * block : (b + d + 1) * block] = piece
                top = jnp.maximum(top, piece)
        at = stale
        for keys in extra(h, i, 0):
            s = lax.dot_general(q, keys, NT, preferred_element_type=F32)
            s_ref[n % 2, :, at : at + keys.shape[0]] = s
            at += keys.shape[0]
            for d in range(0, keys.shape[0], HD):
                top = jnp.maximum(top, s[:, d : d + HD])
        tops[n] = jnp.max(top, axis=1, keepdims=True)

    def weigh(n):
        h, i = steps[n]
        rows = place(i)
        cs = slice(mine + h * HD, mine + (h + 1) * HD)
        top = tops.pop(n)
        if i == 3:
            acc = jnp.zeros((tokens, HD), F32)
            total = jnp.zeros((tokens, 1), F32)
        else:
            before = carry_ref[rows, 2 * mine + 2 * h : 2 * mine + 2 * h + 1]
            top = jnp.maximum(top, before)
            shrink = jnp.exp2((before - top) * SCALE)
            acc = carry_ref[rows, cs] * shrink
            total = carry_ref[rows, 2 * mine + 2 * h + 1 : 2 * mine + 2 * h + 2] * shrink
        top = top * SCALE
        sums = jnp.zeros((tokens, HD), F32)
        values = [pool_ref[b : b + 4, :, cs].reshape(4 * block, HD) for b in range(0, blocks, 4)]
        at = 0
        for v in values + extra(h, i, 1):
            width = v.shape[0]
            w = jnp.exp2(s_ref[n % 2, :, at : at + width] * SCALE - top)
            at += width
            for d in range(0, width, HD):
                sums = sums + w[:, d : d + HD]
            acc = acc + jnp.dot(w.astype(BF16), v, preferred_element_type=F32)
        total = total + jnp.sum(sums, axis=1, keepdims=True)
        outs[parts.index(i)][:, h * HD : (h + 1) * HD] = (acc / total).astype(BF16)

    scores(0)
    for n in range(len(steps)):
        if n + 1 < len(steps):
            scores(n + 1)
        weigh(n)


def unpack(p0, p1, p2, p3, out_ref):
    mine = p0.shape[1]
    for place, ref in zip(peers(), (p0, p1, p2, p3)):
        out_ref[:, pl.ds(pl.multiple_of(place * mine, HD), mine)] = ref[...]


def flips(zh, core):
    pairs = []
    for i in range(math.prod(SIZES)):
        place = list(np.unravel_index(i, SIZES))
        place[3] ^= zh
        place[4] ^= core
        pairs.append((i, int(np.ravel_multi_index(place, SIZES))))
    return pairs


def local(q_fresh, k_fresh, v_fresh, k_stale, v_stale):
    tokens, width = q_fresh.shape
    pooled, mine = k_stale.shape
    heads = mine // HD
    dma = pltpu.SemaphoreType.DMA
    part = jax.ShapeDtypeStruct((tokens, 3 * mine), BF16)
    own, near, same, other, copies = pl.pallas_call(
        pack,
        out_shape=(part,) * 4 + (jax.ShapeDtypeStruct((8, pooled, 2 * mine), BF16),),
        in_specs=[ANY] * 5,
        out_specs=(pl.BlockSpec(),) * 5,
        scratch_shapes=[pltpu.VMEM((tokens, width), BF16)] * 3 + [pltpu.VMEM((pooled, mine), BF16)] * 2 + [dma((5,))],
        compiler_params=pltpu.CompilerParams(vmem_limit_bytes=LIMIT),
        cost_estimate=pl.CostEstimate(flops=0, bytes_accessed=3 << 20, transcendentals=0),
        name="pack",
    )(q_fresh, k_fresh, v_fresh, k_stale, v_stale)
    near = lax.ppermute(near, EVERY, flips(0, 1))
    same = lax.ppermute(same, EVERY, flips(1, 0))
    line = lax.all_to_all(copies, "zl", split_axis=0, concat_axis=0).reshape(8 * pooled, 2 * mine)
    planes = pl.pallas_call(
        spread,
        out_shape=jax.ShapeDtypeStruct((16, 8 * pooled, 2 * mine), BF16),
        in_specs=[VMEM],
        out_specs=ANY,
        scratch_shapes=[dma((16,))],
        compiler_params=pltpu.CompilerParams(vmem_limit_bytes=SPREAD_LIMIT),
        cost_estimate=pl.CostEstimate(flops=0, bytes_accessed=3 << 20, transcendentals=0),
        name="spread",
    )(line)
    other = pl.pallas_call(
        follow,
        out_shape=part,
        in_specs=[ANY, ANY],
        out_specs=ANY,
        input_output_aliases={1: 0},
        compiler_params=pltpu.CompilerParams(vmem_limit_bytes=LIMIT),
        cost_estimate=pl.CostEstimate(flops=0, bytes_accessed=0, transcendentals=0),
        name="follow",
    )(planes, other)
    other = lax.ppermute(other, EVERY, flips(1, 1))
    pool = lax.all_to_all(planes, ("y", "x"), split_axis=0, concat_axis=0)

    early = 3 * tokens
    carry = jax.ShapeDtypeStruct((early, 2 * mine + HD), F32)
    rows = jax.ShapeDtypeStruct((2 * tokens, 2 * mine + HD), F32)
    rows_far = jax.ShapeDtypeStruct((tokens, 2 * mine + HD), F32)
    carry, carry_far, kv = pl.pallas_call(
        attend_early,
        out_shape=(rows, rows_far, jax.ShapeDtypeStruct((early, 2 * mine), BF16)),
        in_specs=[ANY] * 3,
        out_specs=(ANY, ANY, ANY),
        scratch_shapes=[
            pltpu.VMEM((3, tokens, 3 * mine), BF16),
            pltpu.VMEM(carry.shape, F32),
            pltpu.VMEM((2, tokens, early), F32),
            dma((3,)),
            dma((6,)),
        ],
        compiler_params=pltpu.CompilerParams(vmem_limit_bytes=LIMIT),
        cost_estimate=pl.CostEstimate(flops=EARLY_COST, bytes_accessed=3 << 20, transcendentals=0),
        name="attend_early",
    )(own, near, same)
    fresh = 4 * tokens
    total_keys = 16 * 8 * pooled + fresh
    block = jax.ShapeDtypeStruct((tokens, mine), BF16)

    def finish(parts, carry, kv):
        return pl.pallas_call(
            functools.partial(attend, parts),
            out_shape=(block, block),
            in_specs=[VMEM] * 4,
            out_specs=(VMEM, VMEM),
            scratch_shapes=[pltpu.VMEM((2, tokens, total_keys), F32)],
            compiler_params=pltpu.CompilerParams(vmem_limit_bytes=ATTEND_LIMIT),
            cost_estimate=pl.CostEstimate(
                flops=2 * fresh * heads * total_keys * HD,
                bytes_accessed=6 << 20,
                transcendentals=fresh * heads * total_keys // 2,
            ),
            name="attend",
        )(carry, kv, other, pool)

    same, far = finish((2, 3), carry_far, kv)
    first = far
    same = lax.ppermute(same, EVERY, flips(1, 0))
    far = lax.ppermute(far, EVERY, flips(1, 1))
    same, far = pl.pallas_call(
        landed,
        out_shape=(block, block),
        in_specs=[ANY] * 2,
        out_specs=(ANY, ANY),
        input_output_aliases={0: 0, 1: 1},
        compiler_params=pltpu.CompilerParams(vmem_limit_bytes=SPREAD_LIMIT),
        cost_estimate=pl.CostEstimate(flops=EARLY_COST, bytes_accessed=0, transcendentals=0),
        name="landed",
    )(same, far)
    own, near = finish((0, 1), carry, first)
    near = lax.ppermute(near, EVERY, flips(0, 1))
    return pl.pallas_call(
        unpack,
        out_shape=jax.ShapeDtypeStruct((tokens, width), BF16),
        in_specs=[VMEM] * 4,
        out_specs=VMEM,
        compiler_params=pltpu.CompilerParams(vmem_limit_bytes=SPREAD_LIMIT),
        cost_estimate=pl.CostEstimate(flops=0, bytes_accessed=1 << 20, transcendentals=0),
        name="unpack",
    )(own, near, same, far)


def solution(mesh):
    fine = Mesh(mesh.devices.reshape(SIZES), EVERY)
    whole = P(EVERY, None)
    part = P(("y", "x", "zl"), ("zh", "core"))
    return jax.shard_map(
        local,
        mesh=fine,
        in_specs=(whole, whole, whole, part, part),
        out_specs=whole,
        check_vma=False,
    )
```
